32 devices in a mesh: dp: 4 (over z), group: 8 (over y, x, core).
Axes of the slice: x: 2, y: 2, z: 4, core: 2. Of those that a mesh axis runs over, the one named last changes fastest.
Arguments:
- images: bfloat16 [64, 8, 8, 4096], P('dp', None, None, 'group'), may hold values from -6 to 6
- cotangent: bfloat16 [64, 8, 8, 4096], P('dp', None, None, 'group'), may hold values from -6 to 6
- conv_weight: bfloat16 [2, 576, 4096], P(None, 'dp', 'group'), may hold values from -0.25 to 0.25
- mix_weight: bfloat16 [2, 4096, 4096], P(None, 'group', 'dp'), may hold values from -0.09375 to 0.09375
Outputs:
- features_out: bfloat16 [64, 8, 8, 4096], P('dp', None, None, 'group')
- grad_images: bfloat16 [64, 8, 8, 4096], P('dp', None, None, 'group')
- grad_conv: float32 [2, 576, 4096], P(None, 'dp', 'group')
- grad_mix: float32 [2, 4096, 4096], P(None, 'group', 'dp')
The draws below stay inside these ranges and needn't reach their ends.
All inputs are finite; a program needn't handle non-finite values.
Results may differ from the reference program's by a relative error of at most 0.022.
Values may be sent and summed in bfloat16 or wider, within the bound.
No kernel may reach another device: no remote copies, remote signals or barrier semaphores. Data moves between devices by JAX's collectives and lax.ppermute only.
A program may use at most 192 MiB of HBM per device.

```python
import math
import jax
import jax.numpy as jnp
from jax import lax

GROUPS = 64
GW = 64
SIDE = 8
LAYERS = 2
C = 4096
IMAGES = 64
N_GROUP = 8


def block_scale(own_key, extent, split, smallest, high):
    loudness, own = 1.0, jax.random.fold_in(own_key, 6)
    for dim, parts in split:
        heights = jnp.exp(jax.random.uniform(jax.random.fold_in(own, dim), (parts,), jnp.float32, smallest / len(split), high / len(split)))
        loudness = loudness * jnp.repeat(heights, extent[dim] // parts).reshape([-1 if axis == dim else 1 for axis in range(len(extent))])
    return loudness


def centred(key, shape, spread, most, cuts=(), dtype=jnp.bfloat16):
    entries = jax.random.normal(key, shape, jnp.float32) * spread
    if len(cuts) > 0:
        entries = block_scale(key, shape, cuts, -0.22, 0.18) * entries
    return jnp.clip(entries, min=-most, max=most).astype(dtype)


def setup_inputs(seed: int = 0) -> dict:
    splits = jax.random.split(jax.random.key(seed), 5)
    images = centred(splits[0], (IMAGES, SIDE, SIDE, C), 1.0, 6.0, ((0, 4), (3, 8)))
    cotangent = centred(splits[1], (IMAGES, SIDE, SIDE, C), 1.0, 6.0, ((0, 4), (3, 8)))
    conv_weight = centred(splits[2], (LAYERS, 9 * GW, C), (9 * GW) ** -0.5, 0.25, ((1, 4), (2, 8)))
    mix_weight = centred(splits[3], (LAYERS, C, C), C ** -0.5, 0.09375, ((1, 8), (2, 4)))
    return dict(images=images, cotangent=cotangent, conv_weight=conv_weight, mix_weight=mix_weight)


def make_patches(field):
    side_cells = field.shape[1]
    padded = jnp.pad(field, ((0, 0), (1, 1), (1, 1), (0, 0)))
    tap_list = [padded[:, row_shift:row_shift + side_cells, col_shift:col_shift + side_cells, :] for row_shift in range(3) for col_shift in range(3)]
    return jnp.stack(tap_list, axis=3).reshape(-1, 9, field.shape[3])

def fold_patches(pieces, batch_size, side_cells):
    pieces = pieces.reshape(batch_size, side_cells, side_cells, 9, pieces.shape[2])
    summed = jnp.zeros((batch_size, side_cells + 2, side_cells + 2, pieces.shape[4]), jnp.float32)
    for tap_index in range(9):
        row_shift = tap_index // 3
        col_shift = tap_index % 3
        summed = summed + jnp.pad(pieces[:, :, :, tap_index, :], ((0, 0), (row_shift, 2 - row_shift), (col_shift, 2 - col_shift), (0, 0)))
    return summed[:, 1:side_cells + 1, 1:side_cells + 1, :]

def silu_slope(value):
    sigmoid_v = jax.nn.sigmoid(value)
    return sigmoid_v * (1.0 + value * (1.0 - sigmoid_v))

def block_mix(hidden, weight):
    pixel_count, channels = hidden.shape
    block_width = channels // N_GROUP
    hidden_blocks = hidden.reshape(pixel_count, N_GROUP, block_width).transpose(1, 0, 2)
    weight_blocks = weight.reshape(N_GROUP, block_width, channels)

    def add_block(total, pair):
        term = jnp.dot(pair[0], pair[1], preferred_element_type=jnp.float32)
        rounded = lax.optimization_barrier(term.astype(jnp.bfloat16))
        return (total + rounded.astype(jnp.float32), None)
    total, _ = lax.scan(add_block, jnp.zeros((pixel_count, channels), jnp.float32), (hidden_blocks, weight_blocks))
    return total

def reference(images, cotangent, conv_weight, mix_weight):
    image_count, side_cells, _, channels = images.shape
    pixel_count = image_count * side_cells * side_cells
    grad_scale = 1.0 / math.sqrt(pixel_count)

    def split_groups(field):
        return field.reshape(image_count, side_cells, side_cells, GROUPS, GW).transpose(3, 0, 1, 2, 4)

    def merge_groups(stacked):
        return stacked.transpose(1, 0, 2).reshape(pixel_count, channels)

    def conv_one(pair):
        patches = make_patches(pair[0]).reshape(-1, 9 * GW)
        return jnp.dot(patches, pair[1], preferred_element_type=jnp.float32)
    current = images
    saved = []
    for layer in range(LAYERS):
        tap_weights = conv_weight[layer].reshape(9 * GW, GROUPS, GW).transpose(1, 0, 2)
        pre_act = merge_groups(lax.map(conv_one, (split_groups(current), tap_weights)))
        hidden = jax.nn.silu(pre_act).astype(jnp.bfloat16)
        mixed = block_mix(hidden, mix_weight[layer])
        saved.append((current, pre_act, hidden, tap_weights))
        current = (current.reshape(pixel_count, channels).astype(jnp.float32) + mixed).astype(jnp.bfloat16).reshape(images.shape)
    features_out = current

    def back_one(triple):
        patches = make_patches(triple[0]).reshape(-1, 9 * GW)
        weight_term = jnp.dot(patches.T, triple[1], preferred_element_type=jnp.float32)
        patch_term = jnp.dot(triple[1], triple[2].T, preferred_element_type=jnp.float32).reshape(-1, 9, GW)
        return (weight_term, fold_patches(patch_term, image_count, side_cells))
    gradient = cotangent
    conv_grads = []
    mix_grads = []
    for layer in reversed(range(LAYERS)):
        before, pre_act, hidden, tap_weights = saved[layer]
        flat_grad = gradient.reshape(pixel_count, channels)
        grad_mix = jnp.dot(hidden.T, flat_grad, preferred_element_type=jnp.float32) * grad_scale
        grad_hidden = jnp.dot(flat_grad, mix_weight[layer].T, preferred_element_type=jnp.float32)
        grad_pre = (grad_hidden * silu_slope(pre_act)).astype(jnp.bfloat16)
        grad_groups = grad_pre.reshape(pixel_count, GROUPS, GW).transpose(1, 0, 2)
        weight_terms, field_terms = lax.map(back_one, (split_groups(before), grad_groups, tap_weights))
        conv_grad = weight_terms.transpose(1, 0, 2).reshape(9 * GW, channels) * grad_scale
        field_grad = field_terms.transpose(1, 2, 3, 0, 4).reshape(images.shape)
        gradient = (gradient.astype(jnp.float32) + field_grad).astype(jnp.bfloat16)
        conv_grads.insert(0, conv_grad)
        mix_grads.insert(0, grad_mix)
    return (features_out, gradient, jnp.stack(conv_grads), jnp.stack(mix_grads))
```

```python
import functools
import math

import jax
import jax.numpy as jnp
from jax import lax
from jax.experimental import pallas as pl
from jax.experimental.pallas import tpu as pltpu
from jax.sharding import PartitionSpec as P

GW = 64
TAPS = 9
HALF = 256
BF = jnp.bfloat16
F32 = jnp.float32
VMEM_LIMIT = 40 * 1024 * 1024

UP = [(0, 1), (1, 2), (2, 3)]
DOWN = [(3, 2), (2, 1), (1, 0)]
ACROSS_CORE = [(i, i ^ 1) for i in range(8)]
ACROSS_X = [(i, i ^ 2) for i in range(8)]
ACROSS_Y = [(i, i ^ 4) for i in range(8)]


def dot(a, b):
    return jnp.dot(a, b, preferred_element_type=F32)


def dot_nt(a, b):
    return lax.dot_general(a, b, (((1,), (1,)), ((), ())), preferred_element_type=F32)


def call(kernel, out_shape, flops, nbytes, **kw):
    return pl.pallas_call(
        kernel,
        out_shape=out_shape,
        compiler_params=pltpu.CompilerParams(vmem_limit_bytes=VMEM_LIMIT),
        cost_estimate=pl.CostEstimate(flops=flops, bytes_accessed=nbytes, transcendentals=0),
        **kw,
    )


def block_mask():
    rows = lax.broadcasted_iota(jnp.int32, (HALF, HALF), 0) // GW
    cols = lax.broadcasted_iota(jnp.int32, (HALF, HALF), 1) // GW
    return rows == cols


def spread_taps(w_ref, wide_ref, by_rows):
    mask = block_mask()
    for tap in range(TAPS):
        slab = w_ref[tap * GW : (tap + 1) * GW, :]
        square = jnp.concatenate([slab] * (HALF // GW), axis=0)
        square = jnp.where(mask, square, jnp.zeros_like(square))
        if by_rows:
            wide_ref[tap * HALF : (tap + 1) * HALF, :] = square
        else:
            wide_ref[:, tap * HALF : (tap + 1) * HALF] = square


def pad_field(value, pad_ref):
    side = value.shape[0]
    pad_ref[...] = jnp.zeros_like(pad_ref)
    pad_ref[1 : side + 1, 1 : side + 1] = value


def conv_kernel(x_ref, w_ref, hidden_ref, hidden_t_ref, slope_ref, pad_ref, wide_ref):
    side, _, images, _ = x_ref.shape
    pad_field(x_ref[...], pad_ref)
    spread_taps(w_ref, wide_ref, True)
    step = 2
    rows = step * side * images
    for part in range(side // step):
        top = part * step
        patches = jnp.concatenate(
            [
                pad_ref[top + a : top + a + step, b : b + side].reshape(rows, HALF)
                for a in range(3)
                for b in range(3)
            ],
            axis=1,
        )
        pre = dot(patches, wide_ref[...])
        sig = jax.nn.sigmoid(pre)
        hidden = (pre * sig).astype(BF)
        here = slice(part * rows, (part + 1) * rows)
        hidden_ref[here, :] = hidden
        hidden_t_ref[:, here] = hidden.T
        slope_ref[here, :] = sig * (1.0 + pre * (1.0 - sig))


def conv_forward(x, w):
    side, _, images, _ = x.shape
    rows = side * side * images
    return call(
        conv_kernel,
        (
            jax.ShapeDtypeStruct((rows, HALF), BF),
            jax.ShapeDtypeStruct((HALF, rows), BF),
            jax.ShapeDtypeStruct((rows, HALF), F32),
        ),
        2 * rows * HALF * HALF * TAPS,
        rows * HALF * 10,
        scratch_shapes=[
            pltpu.VMEM((side + 2, side + 2, images, HALF), BF),
            pltpu.VMEM((TAPS * HALF, HALF), BF),
        ],
    )(x, w)


def field_kernel(gp_ref, w_ref, g_ref, out_ref, pad_ref, wide_ref):
    side, _, images, _ = gp_ref.shape
    pad_field(gp_ref[...], pad_ref)
    spread_taps(w_ref, wide_ref, False)
    step = 2
    rows = step * side * images
    for part in range(side // step):
        top = part * step
        patches = jnp.concatenate(
            [
                pad_ref[top + 2 - a : top + 2 - a + step, 2 - b : 2 - b + side].reshape(rows, HALF)
                for a in range(3)
                for b in range(3)
            ],
            axis=1,
        )
        field = dot_nt(patches, wide_ref[...])
        here = slice(part * rows, (part + 1) * rows)
        out_ref[here, :] = (g_ref[here, :].astype(F32) + field).astype(BF)


def conv_field(gp, w, g):
    side, _, images, _ = gp.shape
    rows = side * side * images
    return call(
        field_kernel,
        jax.ShapeDtypeStruct((rows, HALF), BF),
        2 * rows * HALF * HALF * TAPS,
        rows * HALF * 6,
        scratch_shapes=[
            pltpu.VMEM((side + 2, side + 2, images, HALF), BF),
            pltpu.VMEM((HALF, TAPS * HALF), BF),
        ],
    )(gp, w, g)


def conv_grad_kernel(x_ref, gp_ref, out_ref, pad_ref):
    side, _, images, _ = x_ref.shape
    rows = side * side * images
    pad_field(x_ref[...], pad_ref)
    turned = gp_ref[...].T
    mask = block_mask()
    for tap in range(TAPS):
        a, b = tap // 3, tap % 3
        square = dot(turned, pad_ref[a : a + side, b : b + side].reshape(rows, HALF)).T
        square = jnp.where(mask, square, 0.0)
        slab = square[:GW]
        for q in range(1, HALF // GW):
            slab = slab + square[q * GW : (q + 1) * GW]
        out_ref[tap * GW : (tap + 1) * GW, :] = slab.astype(BF)


def conv_grad(x, gp):
    side, _, images, _ = x.shape
    rows = side * side * images
    return call(
        conv_grad_kernel,
        jax.ShapeDtypeStruct((TAPS * GW, HALF), BF),
        2 * rows * HALF * HALF * TAPS,
        rows * HALF * 4,
        scratch_shapes=[pltpu.VMEM((side + 2, side + 2, images, HALF), BF)],
    )(x, gp)


def place_vector(z, chip, core):
    return jnp.stack([z, chip, core]).astype(jnp.int32)


def with_place(kernel, grid, in_specs, out_specs, out_shape, flops, nbytes, scratch=()):
    return call(
        kernel,
        out_shape,
        flops,
        nbytes,
        grid_spec=pltpu.PrefetchScalarGridSpec(
            num_scalar_prefetch=1,
            grid=grid,
            in_specs=in_specs,
            out_specs=out_specs,
            scratch_shapes=list(scratch),
        ),
    )


def slot_of(rel, p):
    return (p[0] + 4 - (p[1] ^ rel)) % 4


def mix_columns(place, hidden, weights, other):
    rows, depth = hidden.shape
    width = weights.shape[3]

    def kernel(p, h_ref, w_ref, o_ref):
        del p
        o_ref[0] = dot(h_ref[...], w_ref[0, 0]).astype(BF)

    flip = 1 if other else 0
    return with_place(
        kernel,
        (4,),
        [
            pl.BlockSpec((rows, depth), lambda r, p: (0, 0)),
            pl.BlockSpec((1, 1, depth, width), lambda r, p: (slot_of(r, p), p[2] ^ flip, 0, 0)),
        ],
        pl.BlockSpec((1, rows, width), lambda r, p: (r, 0, 0)),
        jax.ShapeDtypeStruct((4, rows, width), BF),
        8 * rows * depth * width,
        8 * rows * width + 8 * depth * width + 2 * rows * depth,
    )(place, hidden, weights)


def mix_rows(place, h0, h1, w0, w1, other):
    rows, depth = h0.shape
    width = w0.shape[3]

    def kernel(p, ha_ref, hb_ref, wa_ref, wb_ref, o_ref):
        del p
        o_ref[0] = (dot(ha_ref[...], wa_ref[0, 0]) + dot(hb_ref[...], wb_ref[0, 0])).astype(BF)

    flip = 1 if other else 0
    h_spec = pl.BlockSpec((rows, depth), lambda r, p: (0, 0))
    w_spec = pl.BlockSpec((1, 1, depth, width), lambda r, p: (slot_of(r, p), p[2] ^ flip, 0, 0))
    return with_place(
        kernel,
        (4,),
        [h_spec, h_spec, w_spec, w_spec],
        pl.BlockSpec((1, rows, width), lambda r, p: (r, 0, 0)),
        jax.ShapeDtypeStruct((4, rows, width), BF),
        16 * rows * depth * width,
        8 * rows * width + 16 * depth * width + 4 * rows * depth,
    )(place, h0, h1, w0, w1)


def grad_pre_rows(place, wide, weights, slope):
    _, _, rows, width = wide.shape
    depth = weights.shape[2]

    def kernel(p, g_ref, w_ref, s_ref, o_ref, acc):
        step = pl.program_id(0)
        part = dot_nt(g_ref[0, 0], w_ref[0, p[2]]) + dot_nt(g_ref[0, 1], w_ref[0, 1 - p[2]])

        @pl.when(step == 0)
        def _():
            acc[...] = part

        @pl.when(step > 0)
        def _():
            acc[...] += part

        @pl.when(step == 3)
        def _():
            o_ref[...] = (acc[...] * s_ref[...]).astype(BF)

    return with_place(
        kernel,
        (4,),
        [
            pl.BlockSpec((1, 2, rows, width), lambda r, p: (r, 0, 0, 0)),
            pl.BlockSpec((1, 2, depth, width), lambda r, p: (slot_of(r, p), 0, 0, 0)),
            pl.BlockSpec((rows, depth), lambda r, p: (0, 0)),
        ],
        pl.BlockSpec((rows, depth), lambda r, p: (0, 0)),
        jax.ShapeDtypeStruct((rows, depth), BF),
        16 * rows * depth * width,
        16 * (rows + depth) * width + 6 * rows * depth,
        [pltpu.VMEM((rows, depth), F32)],
    )(place, wide, weights, slope)


def grad_pre_columns(place, wide0, wide1, w0, w1, slope):
    _, _, rows, width = wide0.shape
    depth = w0.shape[2]

    def kernel(p, ga_ref, gb_ref, wa_ref, wb_ref, s_ref, o_ref, acc):
        step = pl.program_id(0)
        mine, rest = p[2], 1 - p[2]
        part = dot_nt(ga_ref[0, 0], wa_ref[0, mine]) + dot_nt(ga_ref[0, 1], wa_ref[0, rest])
        part += dot_nt(gb_ref[0, 0], wb_ref[0, mine]) + dot_nt(gb_ref[0, 1], wb_ref[0, rest])

        @pl.when(step == 0)
        def _():
            acc[...] = part

        @pl.when(step > 0)
        def _():
            acc[...] += part

        @pl.when(step == 3)
        def _():
            o_ref[...] = (acc[...] * s_ref[...]).astype(BF)

    g_spec = pl.BlockSpec((1, 2, rows, width), lambda r, p: (r, 0, 0, 0))
    w_spec = pl.BlockSpec((1, 2, depth, width), lambda r, p: (slot_of(r, p), 0, 0, 0))
    return with_place(
        kernel,
        (4,),
        [g_spec, g_spec, w_spec, w_spec, pl.BlockSpec((rows, depth), lambda r, p: (0, 0))],
        pl.BlockSpec((rows, depth), lambda r, p: (0, 0)),
        jax.ShapeDtypeStruct((rows, depth), BF),
        32 * rows * depth * width,
        32 * (rows + depth) * width + 6 * rows * depth,
        [pltpu.VMEM((rows, depth), F32)],
    )(place, wide0, wide1, w0, w1, slope)


def mix_grad(place, hidden_t, wide):
    depth, rows = hidden_t.shape
    width = wide.shape[3]

    def kernel(p, h_ref, g_ref, o_ref):
        o_ref[0, p[2]] = dot(h_ref[...], g_ref[0, 0]).astype(BF)
        o_ref[0, 1 - p[2]] = dot(h_ref[...], g_ref[0, 1]).astype(BF)

    return with_place(
        kernel,
        (4,),
        [
            pl.BlockSpec((depth, rows), lambda i, p: (0, 0)),
            pl.BlockSpec((1, 2, rows, width), lambda i, p: (p[1] ^ ((p[0] + i) % 4), 0, 0, 0)),
        ],
        pl.BlockSpec((1, 2, depth, width), lambda i, p: (i, 0, 0, 0)),
        jax.ShapeDtypeStruct((4, 2, depth, width), BF),
        16 * rows * depth * width,
        16 * (rows + depth) * width + 2 * rows * depth,
    )(place, hidden_t, wide)


def gather_dp(own, z):
    up, down = own, own
    ups, downs = [], []
    for step in range(3):
        up = lax.ppermute(up, "dp", UP[step:])
        down = lax.ppermute(down, "dp", DOWN[step:])
        ups.append(up)
        downs.append(down)
    slots = [own] + [jnp.where(z >= j, ups[j - 1], downs[3 - j]) for j in (1, 2, 3)]
    return jnp.stack(slots)


def scatter_dp(parts):
    up = lax.ppermute(parts[3], "dp", UP[:1])
    down = lax.ppermute(parts[1], "dp", DOWN[:1])
    for step in (2, 3):
        up_term = (parts[4 - step].astype(F32) + up.astype(F32)).astype(BF)
        down_term = (parts[step].astype(F32) + down.astype(F32)).astype(BF)
        up = lax.ppermute(up_term, "dp", UP[:step])
        down = lax.ppermute(down_term, "dp", DOWN[:step])
    return parts[0].astype(F32) + up.astype(F32) + down.astype(F32)


def gather_group(own):
    cut = own.shape[0] // 2
    first, second = own[:cut], own[cut:]
    first = jnp.stack([first, lax.ppermute(first, "group", ACROSS_X)])
    second = jnp.stack([second, lax.ppermute(second, "group", ACROSS_Y)])
    first_y = lax.ppermute(first, "group", ACROSS_Y)
    second_x = lax.ppermute(second, "group", ACROSS_X)
    firsts = jnp.stack([first[0], first[1], first_y[0], first_y[1]])
    seconds = jnp.stack([second[0], second_x[0], second[1], second_x[1]])
    mine = jnp.concatenate([firsts, seconds], axis=1)
    return jnp.stack([mine, lax.ppermute(mine, "group", ACROSS_CORE)], axis=1)


def scatter_group(keep, sent):
    cut = keep.shape[1] // 2
    both = keep.astype(F32) + lax.ppermute(sent, "group", ACROSS_CORE).astype(F32)
    first, second = both[:, :cut], both[:, cut:]
    first_x = lax.ppermute(jnp.stack([first[1], first[3]]).astype(BF), "group", ACROSS_X)
    second_y = lax.ppermute(jnp.stack([second[2], second[3]]).astype(BF), "group", ACROSS_Y)
    first_near = first[0] + first_x[0].astype(F32)
    first_far = first[2] + first_x[1].astype(F32)
    second_near = second[0] + second_y[0].astype(F32)
    second_far = second[1] + second_y[1].astype(F32)
    first_y = lax.ppermute(first_far.astype(BF), "group", ACROSS_Y)
    second_x = lax.ppermute(second_far.astype(BF), "group", ACROSS_X)
    return jnp.concatenate([first_near + first_y.astype(F32), second_near + second_x.astype(F32)])


def staged(images, cotangent, conv_weight, mix_weight):
    batch, side, _, width = images.shape
    rows = batch * side * side
    scale = 1.0 / math.sqrt(rows * lax.axis_size("dp"))
    z = lax.axis_index("dp")
    group = lax.axis_index("group")
    place = place_vector(z, group // 2, group % 2)

    def to_rows(field):
        return field.transpose(1, 2, 0, 3).reshape(rows, width)

    def from_rows(flat):
        return flat.reshape(side, side, batch, width).transpose(2, 0, 1, 3)

    def half(flat, h):
        return flat[:, h * HALF : (h + 1) * HALF]

    def grid_of(flat):
        return flat.reshape(side, side, batch, flat.shape[1])

    conv = [lax.all_gather(conv_weight[layer], "dp", axis=0, tiled=True) for layer in range(2)]
    w0 = mix_weight[0].reshape(width, 2, 2, HALF).transpose(2, 1, 0, 3)
    w1 = mix_weight[1].reshape(2, HALF, 2, width).transpose(0, 2, 1, 3)
    x0 = to_rows(images)
    g2 = to_rows(cotangent)
    w0 = [gather_dp(w0[h], z) for h in range(2)]
    wide2 = gather_group(g2)
    w1 = [gather_dp(w1[h], z) for h in range(2)]

    layer0 = [conv_forward(grid_of(half(x0, h)), half(conv[0], h)) for h in range(2)]
    hidden0 = jnp.concatenate([layer0[0][0], layer0[1][0]], axis=1)
    hidden0_t = jnp.concatenate([layer0[0][1], layer0[1][1]], axis=0)
    slope0 = jnp.concatenate([layer0[0][2], layer0[1][2]], axis=1)

    x1, layer1, mix1 = [], [], []
    for h in range(2):
        sent = mix_columns(place, hidden0, w0[h], True)
        keep = mix_columns(place, hidden0, w0[h], False)
        mixed = scatter_group(keep, sent)
        x1.append((half(x0, h).astype(F32) + mixed).astype(BF))
        layer1.append(conv_forward(grid_of(x1[h]), half(conv[1], h)))
        mix1.append(scatter_dp(mix_grad(place, layer1[h][1], wide2)))

    g1, wide1, mix0, gp1 = [], [], [], []
    for h in range(2):
        gp1.append(grid_of(grad_pre_rows(place, wide2, w1[h], layer1[h][2])))
        g1.append(conv_field(gp1[h], half(conv[1], h), half(g2, h)))
        wide1.append(gather_group(g1[h]))
        mix0.append(scatter_dp(mix_grad(place, hidden0_t, wide1[h])))

    gp0 = grad_pre_columns(place, wide1[0], wide1[1], w0[0], w0[1], slope0)
    conv_terms = [
        jnp.concatenate(
            [conv_grad(grid_of(half(x0, h)), half(gp0, h)) for h in range(2)], axis=1
        ),
        jnp.concatenate(
            [conv_grad(grid_of(x1[h]), gp1[h].reshape(rows, HALF)) for h in range(2)], axis=1
        ),
    ]
    conv_sums = [
        lax.psum_scatter(term, "dp", scatter_dimension=0, tiled=True).astype(F32) * scale
        for term in conv_terms
    ]
    g0 = jnp.concatenate(
        [conv_field(grid_of(half(gp0, h)), half(conv[0], h), half(g1[h], 0)) for h in range(2)],
        axis=1,
    )

    sent = mix_rows(place, layer1[0][0], layer1[1][0], w1[0], w1[1], True)
    keep = mix_rows(place, layer1[0][0], layer1[1][0], w1[0], w1[1], False)
    mixed = scatter_group(keep, sent)
    x2 = (jnp.concatenate(x1, axis=1).astype(F32) + mixed).astype(BF)

    grad_mix0 = jnp.stack(mix0).transpose(2, 1, 0, 3).reshape(width, 2 * width) * scale
    grad_mix1 = jnp.stack(mix1).transpose(0, 2, 1, 3).reshape(width, 2 * width) * scale
    return (
        from_rows(x2),
        from_rows(g0),
        jnp.stack(conv_sums),
        jnp.stack([grad_mix0, grad_mix1]),
    )


def make_patches(field):
    side_cells = field.shape[1]
    padded = jnp.pad(field, ((0, 0), (1, 1), (1, 1), (0, 0)))
    tap_list = [
        padded[:, row_shift : row_shift + side_cells, col_shift : col_shift + side_cells, :]
        for row_shift in range(3)
        for col_shift in range(3)
    ]
    return jnp.stack(tap_list, axis=3).reshape(-1, 9, field.shape[3])


def fold_patches(pieces, batch_size, side_cells):
    pieces = pieces.reshape(batch_size, side_cells, side_cells, 9, pieces.shape[2])
    summed = jnp.zeros((batch_size, side_cells + 2, side_cells + 2, pieces.shape[4]), F32)
    for tap_index in range(9):
        row_shift = tap_index // 3
        col_shift = tap_index % 3
        summed = summed + jnp.pad(
            pieces[:, :, :, tap_index, :],
            ((0, 0), (row_shift, 2 - row_shift), (col_shift, 2 - col_shift), (0, 0)),
        )
    return summed[:, 1 : side_cells + 1, 1 : side_cells + 1, :]


def silu_slope(value):
    sigmoid_v = jax.nn.sigmoid(value)
    return sigmoid_v * (1.0 + value * (1.0 - sigmoid_v))


def general(images, cotangent, conv_weight, mix_weight):
    batch_size, side_cells, _, local_width = images.shape
    local_groups = local_width // GW
    row_count = batch_size * side_cells * side_cells
    layer_count = conv_weight.shape[0]
    grad_scale = 1.0 / math.sqrt(row_count * lax.axis_size("dp"))
    fetched = [
        (
            lax.all_gather(conv_weight[layer], "dp", axis=0, tiled=True),
            lax.all_gather(mix_weight[layer], "dp", axis=1, tiled=True),
        )
        for layer in range(layer_count)
    ]
    current = images
    saved = []
    for layer in range(layer_count):
        conv_full, mix_full = fetched[layer]
        tap_weights = conv_full.reshape(9 * GW, local_groups, GW).transpose(1, 0, 2)
        flat = make_patches(current).reshape(row_count, 9, local_groups, GW)
        patches = flat.transpose(0, 2, 1, 3).reshape(row_count, local_groups, 9 * GW)
        pre_act = jnp.einsum(
            "pgk,gko->pgo", patches, tap_weights, preferred_element_type=F32
        ).reshape(row_count, local_width)
        hidden = jax.nn.silu(pre_act).astype(BF)
        mixed = lax.psum_scatter(
            jnp.dot(hidden, mix_full, preferred_element_type=F32).astype(BF),
            "group",
            scatter_dimension=1,
            tiled=True,
        ).astype(F32)
        saved.append((patches, pre_act, hidden, tap_weights, mix_full))
        current = (
            (current.reshape(row_count, local_width).astype(F32) + mixed)
            .astype(BF)
            .reshape(images.shape)
        )
    gradient = cotangent
    conv_grads = []
    mix_grads = []
    for layer in reversed(range(layer_count)):
        patches, pre_act, hidden, tap_weights, mix_full = saved[layer]
        flat_grad = gradient.reshape(row_count, local_width)
        grad_wide = lax.all_gather(flat_grad, "group", axis=1, tiled=True)
        mix_term = lax.dot_general(
            hidden, grad_wide, (((0,), (0,)), ((), ())), preferred_element_type=F32
        )
        grad_hidden = dot_nt(grad_wide, mix_full)
        grad_pre = (
            (grad_hidden * silu_slope(pre_act)).astype(BF).reshape(row_count, local_groups, GW)
        )
        conv_term = jnp.einsum("pgk,pgo->gko", patches, grad_pre, preferred_element_type=F32)
        conv_term = conv_term.transpose(1, 0, 2).reshape(9 * GW, local_width)
        patch_grad = jnp.einsum("pgo,gko->pgk", grad_pre, tap_weights, preferred_element_type=F32)
        patch_grad = (
            patch_grad.reshape(row_count, local_groups, 9, GW)
            .transpose(0, 2, 1, 3)
            .reshape(row_count, 9, local_width)
        )
        field_grad = fold_patches(patch_grad, batch_size, side_cells)
        conv_summed, mix_summed = (
            lax.psum_scatter(
                conv_term.astype(BF), "dp", scatter_dimension=0, tiled=True
            ).astype(F32),
            lax.psum_scatter(
                mix_term.astype(BF), "dp", scatter_dimension=1, tiled=True
            ).astype(F32),
        )
        conv_grads.insert(0, conv_summed * grad_scale)
        mix_grads.insert(0, mix_summed * grad_scale)
        gradient = (gradient.astype(F32) + field_grad).astype(BF)
    return (current, gradient, jnp.stack(conv_grads), jnp.stack(mix_grads))


def solution(mesh):
    fits = mesh.shape["dp"] == 4 and mesh.shape["group"] == 8
    return jax.shard_map(
        staged if fits else general,
        mesh=mesh,
        in_specs=(
            P("dp", None, None, "group"),
            P("dp", None, None, "group"),
            P(None, "dp", "group"),
            P(None, "group", "dp"),
        ),
        out_specs=(
            P("dp", None, None, "group"),
            P("dp", None, None, "group"),
            P(None, "dp", "group"),
            P(None, "group", "dp"),
        ),
        check_vma=False,
    )
```

```python
import functools
import math

import jax
import jax.numpy as jnp
from jax import lax
from jax.experimental import pallas as pl
from jax.experimental.pallas import tpu as pltpu
from jax.sharding import PartitionSpec as P

GW = 64
TAPS = 9
HALF = 256
BF = jnp.bfloat16
F32 = jnp.float32
MIB = 1024 * 1024

OUTER_INNER = [(0, 1), (1, 0), (2, 3), (3, 2)]
INNER = [(1, 2), (2, 1)]
OUTWARD = [(1, 0), (2, 3)]
INWARD = [(0, 1), (3, 2)]
ACROSS_CORE = [(i, i ^ 1) for i in range(8)]
ACROSS_X = [(i, i ^ 2) for i in range(8)]
ACROSS_Y = [(i, i ^ 4) for i in range(8)]


def dot(a, b):
    return jnp.dot(a, b, preferred_element_type=F32)


def dot_nt(a, b):
    return lax.dot_general(a, b, (((1,), (1,)), ((), ())), preferred_element_type=F32)


def call(kernel, out_shape, flops, nbytes, vmem=24, **kw):
    return pl.pallas_call(
        kernel,
        out_shape=out_shape,
        compiler_params=pltpu.CompilerParams(vmem_limit_bytes=vmem * MIB),
        cost_estimate=pl.CostEstimate(flops=flops, bytes_accessed=nbytes, transcendentals=0),
        **kw,
    )


def block_mask():
    rows = lax.broadcasted_iota(jnp.int32, (HALF, HALF), 0) // GW
    cols = lax.broadcasted_iota(jnp.int32, (HALF, HALF), 1) // GW
    return rows == cols


def spread_taps(w_ref, wide_ref, by_rows):
    mask = block_mask()
    for tap in range(TAPS):
        slab = w_ref[tap * GW : (tap + 1) * GW, :]
        square = jnp.concatenate([slab] * (HALF // GW), axis=0)
        square = jnp.where(mask, square, jnp.zeros_like(square))
        if by_rows:
            wide_ref[tap * HALF : (tap + 1) * HALF, :] = square
        else:
            wide_ref[:, tap * HALF : (tap + 1) * HALF] = square


def pad_field(value, pad_ref):
    side = value.shape[0]
    pad_ref[...] = jnp.zeros_like(pad_ref)
    pad_ref[1 : side + 1, 1 : side + 1] = value


STRIP = 2


def strips(pad_ref, flipped):
    side, images = pad_ref.shape[0] - 2, pad_ref.shape[2]
    rows = STRIP * side * images
    for part in range(side // STRIP):
        top = part * STRIP
        taps = [(2 - a, 2 - b) if flipped else (a, b) for a in range(3) for b in range(3)]
        patches = jnp.concatenate(
            [
                pad_ref[top + a : top + a + STRIP, b : b + side].reshape(rows, HALF)
                for a, b in taps
            ],
            axis=1,
        )
        yield slice(part * rows, (part + 1) * rows), patches


def convolve(x, w_ref, pad_ref, wide_ref, put):
    pad_field(x, pad_ref)
    spread_taps(w_ref, wide_ref, True)
    for here, patches in strips(pad_ref, False):
        pre = dot(patches, wide_ref[...])
        sig = jax.nn.sigmoid(pre)
        put(here, (pre * sig).astype(BF), sig * (1.0 + pre * (1.0 - sig)))


def convolve_back(gp, w_ref, pad_ref, wide_ref, put):
    pad_field(gp, pad_ref)
    spread_taps(w_ref, wide_ref, False)
    for here, patches in strips(pad_ref, True):
        put(here, dot_nt(patches, wide_ref[...]))


def conv_scratch(side, images):
    return [
        pltpu.VMEM((side + 2, side + 2, images, HALF), BF),
        pltpu.VMEM((TAPS * HALF, HALF), BF),
    ]


def place_vector(z, chip, core):
    return jnp.stack([z, chip, core]).astype(jnp.int32)


def with_place(kernel, grid, in_specs, out_specs, out_shape, flops, nbytes, scratch=(), vmem=24):
    return call(
        kernel,
        out_shape,
        flops,
        nbytes,
        vmem,
        grid_spec=pltpu.PrefetchScalarGridSpec(
            num_scalar_prefetch=1,
            grid=grid,
            in_specs=in_specs,
            out_specs=out_specs,
            scratch_shapes=list(scratch),
        ),
    )


def whole(shape):
    return pl.BlockSpec(shape, lambda s, p: (0,) * len(shape))


def rel_chip(slot, p):
    return p[0] ^ p[1] ^ slot


def fill_slots(p, refs, put):
    own, a, b, c, d, e = refs
    inner = (p[0] == 1) | (p[0] == 2)
    put(0, own)
    put(1, a)

    @pl.when(inner)
    def _():
        put(2, c)
        put(3, b)

    @pl.when(jnp.logical_not(inner))
    def _():
        put(2, d)
        put(3, e)


def put_columns(p, refs, sel, start, depth):
    width = sel.shape[3]

    def put(j, ref):
        sel[0, j, start : start + depth] = ref[:depth, :width]
        sel[1, j, start : start + depth] = ref[:depth, width:]

    fill_slots(p, refs, put)


def put_kernels(p, refs, conv, depth, tall):
    width = conv.shape[1]
    shard = conv.shape[0] // 4

    def put(j, ref):
        start = pl.multiple_of((p[0] ^ j) * shard, 16)
        conv[pl.ds(start, tall), :] = ref[depth : depth + tall, :width]
        start = pl.multiple_of((p[0] ^ j) * shard + shard - tall, 16)
        conv[pl.ds(start, tall), :] = ref[depth : depth + tall, width:]

    fill_slots(p, refs, put)


def first_layer(place, x, piece, side):
    rows, width = x.shape
    images = rows // (side * side)

    def kernel(p, x_ref, *refs):
        sent, keep, hid_t, slope, conv, hid, sel, pad_ref, wide_ref = refs[6:]
        step = pl.program_id(0)

        @pl.when(step == 0)
        def _():
            put_kernels(p, refs[:6], conv, width, piece[0].shape[0] - width)
            put_columns(p, refs[:6], sel, 0, width)
            for h in range(width // HALF):
                lanes = slice(h * HALF, (h + 1) * HALF)

                def put(here, value, slant, lanes=lanes):
                    hid[here, lanes] = value
                    hid_t[lanes, here] = value.T
                    slope[here, lanes] = slant

                grid = x_ref[:, lanes].reshape(side, side, images, HALF)
                convolve(grid, conv.at[:, lanes], pad_ref, wide_ref, put)

        sent[0] = dot(hid[...], sel[1 - p[2], step]).astype(BF)
        keep[0] = dot(hid[...], sel[p[2], step]).astype(BF)

    mix_spec = pl.BlockSpec((1, rows, width), lambda s, p: (rel_chip(s, p), 0, 0))
    mix_shape = jax.ShapeDtypeStruct((4, rows, width), BF)
    return with_place(
        kernel,
        (4,),
        [whole((rows, width))] + [whole(piece[0].shape)] * 6,
        (mix_spec, mix_spec, whole((width, rows)), whole((rows, width)), whole((TAPS * GW, width))),
        (
            mix_shape,
            mix_shape,
            jax.ShapeDtypeStruct((width, rows), BF),
            jax.ShapeDtypeStruct((rows, width), F32),
            jax.ShapeDtypeStruct((TAPS * GW, width), BF),
        ),
        16 * rows * width * width + 2 * rows * HALF * width * TAPS,
        30 * rows * width,
        [pltpu.VMEM((rows, width), BF), pltpu.VMEM((2, 4, width, width), BF)]
        + conv_scratch(side, images),
        60,
    )(place, x, *piece)


def next_layer(place, base, keep, other, first_x, second_y, first_y, second_x, piece, start, wide, side):
    rows, width = base.shape
    images = rows // (side * side)
    cut = rows // 2

    def kernel(p, b_ref, k_ref, o_ref, fx, sy, fy, sx, *refs):
        g_ref = refs[6]
        x_ref, hid, slope, conv, term = refs[7:12]
        hid_t, pad_ref, wide_ref = refs[12:]
        step = pl.program_id(0)

        @pl.when(step == 0)
        def _():
            put_kernels(p, refs[:6], conv, 0, tall)
            near, far = slice(0, cut), slice(cut, rows)
            x_ref[near, :] = (
                add(b_ref[near, :]) + add(k_ref[0, near, :], o_ref[0, near, :], fx[0], fy[...])
            ).astype(BF)
            x_ref[far, :] = (
                add(b_ref[far, :]) + add(k_ref[0, far, :], o_ref[0, far, :], sy[0], sx[...])
            ).astype(BF)
            for h in range(width // HALF):
                lanes = slice(h * HALF, (h + 1) * HALF)

                def put(here, value, slant, lanes=lanes):
                    hid[here, lanes] = value
                    hid_t[lanes, here] = value.T
                    slope[here, lanes] = slant

                grid = x_ref[:, lanes].reshape(side, side, images, HALF)
                convolve(grid, conv.at[:, lanes], pad_ref, wide_ref, put)

        term[0, :, :width] = dot(hid_t[...], g_ref[0]).astype(BF)
        term[0, :, width:] = dot(hid_t[...], g_ref[1]).astype(BF)

    all_spec = whole((rows, width))
    part = whole((1, rows, width))
    tall = piece[0].shape[0] - start
    block = math.gcd(start, 128)
    return with_place(
        kernel,
        (4,),
        [
            all_spec,
            part,
            part,
            whole((1, cut, width)),
            whole((1, cut, width)),
            whole((cut, width)),
            whole((cut, width)),
        ]
        + [pl.BlockSpec((block, 2 * width), lambda s, p: (start // block, 0))] * 6
        + [pl.BlockSpec((2, rows, width), lambda c, p: (c, 0, 0))],
        (
            all_spec,
            all_spec,
            all_spec,
            whole((TAPS * GW, width)),
            pl.BlockSpec((1, width, 2 * width), lambda c, p: (c, 0, 0)),
        ),
        (
            jax.ShapeDtypeStruct((rows, width), BF),
            jax.ShapeDtypeStruct((rows, width), BF),
            jax.ShapeDtypeStruct((rows, width), F32),
            jax.ShapeDtypeStruct((TAPS * GW, width), BF),
            jax.ShapeDtypeStruct((4, width, 2 * width), BF),
        ),
        16 * rows * width * width + 2 * rows * HALF * width * TAPS,
        32 * rows * width,
        [pltpu.VMEM((width, rows), BF)] + conv_scratch(side, images),
        60,
    )(place, base, keep, other, first_x, second_y, first_y, second_x, *piece, wide)


def output_gradient(place, wide, pieces, slope, conv, gradient, side):
    _, rows, width = wide.shape
    images = rows // (side * side)
    count = len(pieces)
    depth = width // count

    def kernel(p, s_ref, g_ref, *refs):
        c_ref, b_ref, gp_ref, o_ref, acc, sel, pad_ref, wide_ref = refs[6 * count :]
        step = pl.program_id(0)

        @pl.when(step == 0)
        def _():
            for k in range(count):
                put_columns(p, refs[6 * k : 6 * k + 6], sel, k * depth, depth)

        part = dot_nt(g_ref[0], sel[0, step]) + dot_nt(g_ref[1], sel[1, step])

        @pl.when(step == 0)
        def _():
            acc[...] = part

        @pl.when((step > 0) & (step < 3))
        def _():
            acc[...] += part

        @pl.when(step == 3)
        def _():
            gp_ref[...] = ((acc[...] + part) * s_ref[...]).astype(BF)
            for h in range(width // HALF):
                lanes = slice(h * HALF, (h + 1) * HALF)

                def put(here, field, lanes=lanes):
                    o_ref[here, lanes] = (b_ref[here, lanes].astype(F32) + field).astype(BF)

                grid = gp_ref[:, lanes].reshape(side, side, images, HALF)
                convolve_back(grid, c_ref.at[:, lanes], pad_ref, wide_ref, put)

    all_spec = whole((rows, width))
    return with_place(
        kernel,
        (4,),
        [all_spec, pl.BlockSpec((2, rows, width), lambda s, p: (p[0] ^ s, 0, 0))]
        + [whole((depth, 2 * width))] * (6 * count)
        + [whole((TAPS * GW, width)), all_spec],
        (all_spec, all_spec),
        (jax.ShapeDtypeStruct((rows, width), BF), jax.ShapeDtypeStruct((rows, width), BF)),
        16 * rows * width * width + 2 * rows * HALF * width * TAPS,
        32 * rows * width,
        [
            pltpu.VMEM((rows, width), F32),
            pltpu.VMEM((2, 4, width, width), BF),
            pltpu.VMEM((side + 2, side + 2, images, HALF), BF),
            pltpu.VMEM((HALF, TAPS * HALF), BF),
        ],
        60,
    )(place, slope, wide, *[a for piece in pieces for a in piece], conv, gradient)


def mix_columns(place, hidden, pieces):
    rows, width = hidden.shape
    count = len(pieces)
    depth = width // count

    def kernel(p, h_ref, *refs):
        sent, keep, sel = refs[6 * count :]
        step = pl.program_id(0)

        @pl.when(step == 0)
        def _():
            for k in range(count):
                put_columns(p, refs[6 * k : 6 * k + 6], sel, k * depth, depth)

        sent[0] = dot(h_ref[...], sel[1 - p[2], step]).astype(BF)
        keep[0] = dot(h_ref[...], sel[p[2], step]).astype(BF)

    mix_spec = pl.BlockSpec((1, rows, width), lambda s, p: (rel_chip(s, p), 0, 0))
    mix_shape = jax.ShapeDtypeStruct((4, rows, width), BF)
    return with_place(
        kernel,
        (4,),
        [whole(hidden.shape)] + [whole((depth, 2 * width))] * (6 * count),
        (mix_spec, mix_spec),
        (mix_shape, mix_shape),
        16 * rows * width * width,
        32 * rows * width,
        [pltpu.VMEM((2, 4, width, width), BF)],
        48,
    )(place, hidden, *[a for piece in pieces for a in piece])


def grad_pre(place, wide, piece, slope):
    rows, width = slope.shape

    def kernel(p, s_ref, mine_ref, other_ref, *refs):
        o_ref, sel, acc = refs[6:]
        step = pl.program_id(0)

        @pl.when(step == 0)
        def _():
            put_columns(p, refs[:6], sel, 0, width)

        part = dot_nt(mine_ref[0], sel[p[2], step]) + dot_nt(other_ref[0], sel[1 - p[2], step])

        @pl.when(step == 0)
        def _():
            acc[...] = part

        @pl.when((step > 0) & (step < 3))
        def _():
            acc[...] += part

        @pl.when(step == 3)
        def _():
            o_ref[...] = ((acc[...] + part) * s_ref[...]).astype(BF)

    return with_place(
        kernel,
        (4,),
        [whole((rows, width))]
        + [pl.BlockSpec((1, rows, width), lambda s, p: (rel_chip(s, p), 0, 0))] * 2
        + [whole((width, 2 * width))] * 6,
        whole((rows, width)),
        jax.ShapeDtypeStruct((rows, width), BF),
        16 * rows * width * width,
        32 * rows * width,
        [pltpu.VMEM((2, 4, width, width), BF), pltpu.VMEM((rows, width), F32)],
        60,
    )(place, slope, *wide, *piece)


def mix_grad(place, hidden_t, wide, extra=None):
    depth, rows = hidden_t.shape
    width = wide[0].shape[2]
    below = 0 if extra is None else extra.shape[1]

    def kernel(p, h_ref, mine_ref, other_ref, *refs):
        term = refs[-1]
        here = pl.multiple_of(p[2] * width, width)
        there = pl.multiple_of((1 - p[2]) * width, width)
        term[0, :depth, pl.ds(here, width)] = dot(h_ref[...], mine_ref[0]).astype(BF)
        term[0, :depth, pl.ds(there, width)] = dot(h_ref[...], other_ref[0]).astype(BF)
        if below:
            term[0, depth:, :] = refs[0][0]

    g_spec = pl.BlockSpec((1, rows, width), lambda c, p: (p[1] ^ c, 0, 0))
    specs = [whole((depth, rows)), g_spec, g_spec]
    args = [hidden_t, *wide]
    if below:
        specs.append(pl.BlockSpec((1, below, 2 * width), lambda c, p: (c, 0, 0)))
        args.append(extra)
    return with_place(
        kernel,
        (4,),
        specs,
        pl.BlockSpec((1, depth + below, 2 * width), lambda c, p: (c, 0, 0)),
        jax.ShapeDtypeStruct((4, depth + below, 2 * width), BF),
        16 * rows * depth * width,
        16 * (rows + depth) * width + 2 * rows * depth,
        (),
        60,
    )(place, *args)


def conv_grad(place, x, gp, shard, side, relative):
    rows, width = x.shape
    images = rows // (side * side)

    def kernel(p, x_ref, gp_ref, o_ref, pad_ref, full_ref):
        mask = block_mask()
        for k in range(width // HALF):
            lanes = slice(k * HALF, (k + 1) * HALF)
            pad_field(x_ref[:, lanes].reshape(side, side, images, HALF), pad_ref)
            turned = gp_ref[:, lanes].T
            for tap in range(TAPS):
                a, b = tap // 3, tap % 3
                square = dot(turned, pad_ref[a : a + side, b : b + side].reshape(rows, HALF)).T
                square = jnp.where(mask, square, 0.0)
                slab = square[:GW]
                for q in range(1, HALF // GW):
                    slab = slab + square[q * GW : (q + 1) * GW]
                full_ref[tap * GW : (tap + 1) * GW, lanes] = slab.astype(BF)
        for plane in range(4):
            index = plane ^ p[0] if relative else plane
            o_ref[index] = full_ref[plane * shard : (plane + 1) * shard, :]

    return with_place(
        kernel,
        (1,),
        [whole((rows, width))] * 2,
        whole((4, shard, width)),
        jax.ShapeDtypeStruct((4, shard, width), BF),
        2 * rows * HALF * width * TAPS,
        rows * width * 4,
        [
            pltpu.VMEM((side + 2, side + 2, images, HALF), BF),
            pltpu.VMEM((4 * shard, width), BF),
        ],
    )(place, x, gp)


def conv_field(gp, w, gradient, side):
    rows, width = gp.shape
    images = rows // (side * side)

    def kernel(gp_ref, w_ref, g_ref, o_ref, pad_ref, wide_ref):
        def put(here, field):
            o_ref[here, :] = (g_ref[here, :].astype(F32) + field).astype(BF)

        grid = gp_ref[...].reshape(side, side, images, HALF)
        convolve_back(grid, w_ref, pad_ref, wide_ref, put)

    half_spec = pl.BlockSpec((rows, HALF), lambda h: (0, h))
    return call(
        kernel,
        jax.ShapeDtypeStruct((rows, width), BF),
        2 * rows * HALF * width * TAPS,
        rows * width * 6,
        grid=(width // HALF,),
        in_specs=[half_spec, pl.BlockSpec((TAPS * GW, HALF), lambda h: (0, h)), half_spec],
        out_specs=half_spec,
        scratch_shapes=[
            pltpu.VMEM((side + 2, side + 2, images, HALF), BF),
            pltpu.VMEM((HALF, TAPS * HALF), BF),
        ],
    )(gp, w, gradient)


def finish(place, scale, last, first, convs, mix_shape, conv_shape):
    layers, depth, width = mix_shape
    _, shard, channels = conv_shape

    def kernel(p, last_ref, first_ref, *refs):
        del p
        mix_ref, conv_ref = refs[-2:]
        mix_ref[1] = last_ref[0].astype(F32) * scale
        mix_ref[0] = first_ref[0, :depth].astype(F32) * scale
        conv_ref[1, : shard // 2] = first_ref[0, depth:, :channels].astype(F32) * scale
        conv_ref[1, shard // 2 :] = first_ref[0, depth:, channels:].astype(F32) * scale
        total = refs[0][0].astype(F32)
        for ref in refs[1:4]:
            total = total + ref[...].astype(F32)
        conv_ref[0] = total * scale

    return with_place(
        kernel,
        (1,),
        [whole((1, depth, width)), whole((1, depth + shard // 2, width)), whole((1, shard, channels))]
        + [whole((shard, channels))] * 3,
        (whole(mix_shape), whole(conv_shape)),
        (jax.ShapeDtypeStruct(mix_shape, F32), jax.ShapeDtypeStruct(conv_shape, F32)),
        0,
        12 * depth * width,
        (),
        32,
    )(place, last, first, *convs)


class Clock:
    def __init__(self, token):
        self.token = token

    def gate(self, value):
        return lax.optimization_barrier((value, self.token))[0]

    def close(self, *values):
        self.token, *values = lax.optimization_barrier((self.token, *values))
        return values


def permute_dp(value, pairs):
    return lax.ppermute(value, "dp", pairs)


def permute_group(value, pairs):
    return lax.ppermute(value, "group", pairs)


def add(*terms):
    total = terms[0].astype(F32)
    for term in terms[1:]:
        total = total + term.astype(F32)
    return total


def gather_outer(own):
    return permute_dp(own, OUTER_INNER)


def gather_inner(own):
    return permute_dp(own, INNER)


def gather_second(a, b):
    return permute_dp(a, INNER), permute_dp(b, OUTWARD)


def gather_third(c):
    return permute_dp(c, OUTWARD)


def scatter_direct(parts):
    return [permute_dp(parts[i], [(j, j ^ i) for j in range(4)]) for i in (1, 2, 3)]


def plane_first(own):
    cut = own.shape[0] // 2
    return permute_group(own[:cut], ACROSS_X), permute_group(own[cut:], ACROSS_Y)


def plane_second(own, first_x, second_y):
    cut = own.shape[0] // 2
    return (
        permute_group(jnp.stack([own[:cut], first_x]), ACROSS_Y),
        permute_group(jnp.stack([own[cut:], second_y]), ACROSS_X),
    )


def plane_join(own, first_x, second_y, first_y, second_x):
    return jnp.stack(
        [
            own,
            jnp.concatenate([first_x, second_x[0]]),
            jnp.concatenate([first_y[0], second_y]),
            jnp.concatenate([first_y[1], second_x[1]]),
        ]
    )


def across_cores(value):
    return permute_group(value, ACROSS_CORE)


def sum_last(base, keep, other, first_x, second_y, first_y, second_x):
    cut = base.shape[0] // 2
    return jnp.concatenate(
        [
            add(base[:cut]) + add(keep[0, :cut], other[0, :cut], first_x[0], first_y),
            add(base[cut:]) + add(keep[0, cut:], other[0, cut:], second_y[0], second_x),
        ]
    ).astype(BF)


def sum_first(keep, other):
    rows = keep.shape[1]
    cut = rows // 2
    first = [add(keep[c, :cut], other[c, :cut]).astype(BF) for c in (1, 3)]
    second = [add(keep[c, cut:], other[c, cut:]).astype(BF) for c in (2, 3)]
    return (
        permute_group(jnp.stack(first), ACROSS_X),
        permute_group(jnp.stack(second), ACROSS_Y),
    )


def sum_second(keep, other, first_x, second_y):
    cut = keep.shape[1] // 2
    return (
        permute_group(add(keep[2, :cut], other[2, :cut], first_x[1]).astype(BF), ACROSS_Y),
        permute_group(add(keep[1, cut:], other[1, cut:], second_y[1]).astype(BF), ACROSS_X),
    )


def staged(images, cotangent, conv_weight, mix_weight):
    batch, side, _, width = images.shape
    shard = conv_weight.shape[1]
    rows = batch * side * side
    scale = 1.0 / math.sqrt(rows * lax.axis_size("dp"))
    z = lax.axis_index("dp")
    group = lax.axis_index("group")
    place = place_vector(z, group // 2, group % 2)
    clock = Clock(z)
    gate, close = clock.gate, clock.close

    def to_rows(field):
        return field.transpose(1, 2, 0, 3).reshape(rows, width)

    def from_rows(flat):
        return flat.reshape(side, side, batch, width).transpose(2, 0, 1, 3)

    tall = (shard // 2 + 15) // 16 * 16

    def with_kernels(weights, layer):
        kernels = conv_weight[layer]
        below = jnp.concatenate([kernels[:tall], kernels[shard - tall :]], axis=1)
        return jnp.concatenate([weights, below])

    depth = width // 2
    own0 = with_kernels(mix_weight[0], 0)
    own1, own2 = with_kernels(mix_weight[1, :depth], 1), mix_weight[1, depth:]
    a0, b0 = gather_outer(own0), gather_inner(own0)
    x0 = to_rows(images)
    a0, b0, x0 = close(a0, b0, x0)

    g2 = to_rows(gate(cotangent))
    wide2 = lax.all_gather(g2, "group", axis=0)
    c0, d0 = gather_second(a0, b0)
    c0, d0 = close(c0, d0)

    e0 = gather_third(c0)
    b1, b2 = gather_inner(gate(own1)), gather_inner(gate(own2))
    e0, b1, b2 = close(e0, b1, b2)
    p0 = (own0, a0, b0, c0, d0, e0)

    a1 = gather_outer(gate(own1))
    sent, keep, hidden0_t, slope0, conv0 = first_layer(place, x0, p0, side)
    a1, sent, keep, hidden0_t, slope0, conv0 = close(a1, sent, keep, hidden0_t, slope0, conv0)

    a2 = gather_outer(gate(own2))
    other = across_cores(sent)
    a2, other = close(a2, other)

    c1, d1 = gather_second(a1, b1)
    c2, d2 = gather_second(a2, b2)
    sx, sy = sum_first(keep, other)
    c1, d1, c2, d2, sx, sy = close(c1, d1, c2, d2, sx, sy)

    e1 = gather_third(c1)
    ty, tx = sum_second(keep, other, sx, sy)
    ty, tx, e1 = close(ty, tx, e1)
    p1 = (own1, a1, b1, c1, d1, e1)

    e2 = gather_third(gate(c2))
    x1, hidden1, slope1, conv1, m1 = next_layer(
        place, x0, keep, other, sx, sy, ty, tx, p1, depth, wide2, side
    )
    x1, hidden1, slope1, conv1, m1, e2 = close(x1, hidden1, slope1, conv1, m1, e2)
    p2 = (own2, a2, b2, c2, d2, e2)
    last = lax.psum_scatter(m1, "dp", scatter_dimension=0, tiled=True)

    gp1, g1 = output_gradient(place, wide2, [p1, p2], slope1, conv1, g2, side)
    ax, ay = plane_first(g1)
    gp1, g1, ax, ay = close(gp1, g1, ax, ay)
    ayy, axx = plane_second(g1, ax, ay)
    mine = plane_join(g1, ax, ay, ayy, axx)
    terms1 = conv_grad(place, x1, gp1, shard, side, False)
    mine, terms1 = close(mine, terms1)
    wide1 = (mine, across_cores(mine))
    below = jnp.concatenate([terms1[:, : shard // 2], terms1[:, shard // 2 :]], axis=2)
    m0 = mix_grad(place, hidden0_t, wide1, below)
    m0, last = close(m0, last)
    first = lax.psum_scatter(m0, "dp", scatter_dimension=0, tiled=True)

    gp0 = grad_pre(place, wide1, p0, slope0)
    terms0 = conv_grad(place, x0, gp0, shard, side, True)
    gp0, terms0 = close(gp0, terms0)
    cs = scatter_direct(terms0)

    sent, keep = mix_columns(place, gate(hidden1), [p1, p2])
    other = across_cores(sent)
    keep, other = close(keep, other)
    sx, sy = sum_first(keep, other)
    g0 = conv_field(gp0, conv0, g1, side)
    sx, sy, g0, *cs = close(sx, sy, g0, *cs)
    ty, tx = sum_second(keep, other, sx, sy)
    features = from_rows(sum_last(x1, keep, other, sx, sy, ty, tx))
    grad_images = from_rows(g0)
    grad_mix, grad_conv = finish(
        place, scale, last, first, [terms0, *cs], mix_weight.shape, conv_weight.shape
    )
    return features, grad_images, grad_conv, grad_mix


def make_patches(field):
    side_cells = field.shape[1]
    padded = jnp.pad(field, ((0, 0), (1, 1), (1, 1), (0, 0)))
    tap_list = [
        padded[:, row_shift : row_shift + side_cells, col_shift : col_shift + side_cells, :]
        for row_shift in range(3)
        for col_shift in range(3)
    ]
    return jnp.stack(tap_list, axis=3).reshape(-1, 9, field.shape[3])


def fold_patches(pieces, batch_size, side_cells):
    pieces = pieces.reshape(batch_size, side_cells, side_cells, 9, pieces.shape[2])
    summed = jnp.zeros((batch_size, side_cells + 2, side_cells + 2, pieces.shape[4]), F32)
    for tap_index in range(9):
        row_shift = tap_index // 3
        col_shift = tap_index % 3
        summed = summed + jnp.pad(
            pieces[:, :, :, tap_index, :],
            ((0, 0), (row_shift, 2 - row_shift), (col_shift, 2 - col_shift), (0, 0)),
        )
    return summed[:, 1 : side_cells + 1, 1 : side_cells + 1, :]


def silu_slope(value):
    sigmoid_v = jax.nn.sigmoid(value)
    return sigmoid_v * (1.0 + value * (1.0 - sigmoid_v))


def general(images, cotangent, conv_weight, mix_weight):
    batch_size, side_cells, _, local_width = images.shape
    local_groups = local_width // GW
    row_count = batch_size * side_cells * side_cells
    layer_count = conv_weight.shape[0]
    grad_scale = 1.0 / math.sqrt(row_count * lax.axis_size("dp"))
    fetched = [
        (
            lax.all_gather(conv_weight[layer], "dp", axis=0, tiled=True),
            lax.all_gather(mix_weight[layer], "dp", axis=1, tiled=True),
        )
        for layer in range(layer_count)
    ]
    current = images
    saved = []
    for layer in range(layer_count):
        conv_full, mix_full = fetched[layer]
        tap_weights = conv_full.reshape(9 * GW, local_groups, GW).transpose(1, 0, 2)
        flat = make_patches(current).reshape(row_count, 9, local_groups, GW)
        patches = flat.transpose(0, 2, 1, 3).reshape(row_count, local_groups, 9 * GW)
        pre_act = jnp.einsum(
            "pgk,gko->pgo", patches, tap_weights, preferred_element_type=F32
        ).reshape(row_count, local_width)
        hidden = jax.nn.silu(pre_act).astype(BF)
        mixed = lax.psum_scatter(
            jnp.dot(hidden, mix_full, preferred_element_type=F32).astype(BF),
            "group",
            scatter_dimension=1,
            tiled=True,
        ).astype(F32)
        saved.append((patches, pre_act, hidden, tap_weights, mix_full))
        current = (
            (current.reshape(row_count, local_width).astype(F32) + mixed)
            .astype(BF)
            .reshape(images.shape)
        )
    gradient = cotangent
    conv_grads = []
    mix_grads = []
    for layer in reversed(range(layer_count)):
        patches, pre_act, hidden, tap_weights, mix_full = saved[layer]
        flat_grad = gradient.reshape(row_count, local_width)
        grad_wide = lax.all_gather(flat_grad, "group", axis=1, tiled=True)
        mix_term = lax.dot_general(
            hidden, grad_wide, (((0,), (0,)), ((), ())), preferred_element_type=F32
        )
        grad_hidden = dot_nt(grad_wide, mix_full)
        grad_pre = (
            (grad_hidden * silu_slope(pre_act)).astype(BF).reshape(row_count, local_groups, GW)
        )
        conv_term = jnp.einsum("pgk,pgo->gko", patches, grad_pre, preferred_element_type=F32)
        conv_term = conv_term.transpose(1, 0, 2).reshape(9 * GW, local_width)
        patch_grad = jnp.einsum("pgo,gko->pgk", grad_pre, tap_weights, preferred_element_type=F32)
        patch_grad = (
            patch_grad.reshape(row_count, local_groups, 9, GW)
            .transpose(0, 2, 1, 3)
            .reshape(row_count, 9, local_width)
        )
        field_grad = fold_patches(patch_grad, batch_size, side_cells)
        conv_summed, mix_summed = (
            lax.psum_scatter(
                conv_term.astype(BF), "dp", scatter_dimension=0, tiled=True
            ).astype(F32),
            lax.psum_scatter(
                mix_term.astype(BF), "dp", scatter_dimension=1, tiled=True
            ).astype(F32),
        )
        conv_grads.insert(0, conv_summed * grad_scale)
        mix_grads.insert(0, mix_summed * grad_scale)
        gradient = (gradient.astype(F32) + field_grad).astype(BF)
    return (current, gradient, jnp.stack(conv_grads), jnp.stack(mix_grads))


def solution(mesh):
    fits = mesh.shape["dp"] == 4 and mesh.shape["group"] == 8
    return jax.shard_map(
        staged if fits else general,
        mesh=mesh,
        in_specs=(
            P("dp", None, None, "group"),
            P("dp", None, None, "group"),
            P(None, "dp", "group"),
            P(None, "group", "dp"),
        ),
        out_specs=(
            P("dp", None, None, "group"),
            P("dp", None, None, "group"),
            P(None, "dp", "group"),
            P(None, "group", "dp"),
        ),
        check_vma=False,
    )
```

```python
import functools
import math

import jax
import jax.numpy as jnp
from jax import lax
from jax.experimental import pallas as pl
from jax.experimental.pallas import tpu as pltpu
from jax.sharding import PartitionSpec as P

GW = 64
TAPS = 9
HALF = 256
BF = jnp.bfloat16
F32 = jnp.float32
MIB = 1024 * 1024

OUTER_INNER = [(0, 1), (1, 0), (2, 3), (3, 2)]
INNER = [(1, 2), (2, 1)]
OUTWARD = [(1, 0), (2, 3)]
INWARD = [(0, 1), (3, 2)]
ACROSS_CORE = [(i, i ^ 1) for i in range(8)]
ACROSS_X = [(i, i ^ 2) for i in range(8)]
ACROSS_Y = [(i, i ^ 4) for i in range(8)]


def dot(a, b):
    return jnp.dot(a, b, preferred_element_type=F32)


def dot_nt(a, b):
    return lax.dot_general(a, b, (((1,), (1,)), ((), ())), preferred_element_type=F32)


def call(kernel, out_shape, flops, nbytes, vmem=24, **kw):
    return pl.pallas_call(
        kernel,
        out_shape=out_shape,
        compiler_params=pltpu.CompilerParams(vmem_limit_bytes=vmem * MIB),
        cost_estimate=pl.CostEstimate(flops=flops, bytes_accessed=nbytes, transcendentals=0),
        **kw,
    )


def block_mask():
    rows = lax.broadcasted_iota(jnp.int32, (HALF, HALF), 0) // GW
    cols = lax.broadcasted_iota(jnp.int32, (HALF, HALF), 1) // GW
    return rows == cols


def spread_taps(w_ref, wide_ref, by_rows):
    mask = block_mask()
    for tap in range(TAPS):
        slab = w_ref[tap * GW : (tap + 1) * GW, :]
        square = jnp.concatenate([slab] * (HALF // GW), axis=0)
        square = jnp.where(mask, square, jnp.zeros_like(square))
        if by_rows:
            wide_ref[tap * HALF : (tap + 1) * HALF, :] = square
        else:
            wide_ref[:, tap * HALF : (tap + 1) * HALF] = square


def pad_field(value, pad_ref):
    side = value.shape[0]
    pad_ref[...] = jnp.zeros_like(pad_ref)
    pad_ref[1 : side + 1, 1 : side + 1] = value


STRIP = 2


def strips(pad_ref, flipped):
    side, images = pad_ref.shape[0] - 2, pad_ref.shape[2]
    rows = STRIP * side * images
    for part in range(side // STRIP):
        top = part * STRIP
        taps = [(2 - a, 2 - b) if flipped else (a, b) for a in range(3) for b in range(3)]
        patches = jnp.concatenate(
            [
                pad_ref[top + a : top + a + STRIP, b : b + side].reshape(rows, HALF)
                for a, b in taps
            ],
            axis=1,
        )
        yield slice(part * rows, (part + 1) * rows), patches


def convolve(x, w_ref, pad_ref, wide_ref, put):
    pad_field(x, pad_ref)
    spread_taps(w_ref, wide_ref, True)
    for here, patches in strips(pad_ref, False):
        pre = dot(patches, wide_ref[...])
        sig = jax.nn.sigmoid(pre)
        put(here, (pre * sig).astype(BF), sig * (1.0 + pre * (1.0 - sig)))


def convolve_back(gp, w_ref, pad_ref, wide_ref, put):
    pad_field(gp, pad_ref)
    spread_taps(w_ref, wide_ref, False)
    for here, patches in strips(pad_ref, True):
        put(here, dot_nt(patches, wide_ref[...]))


def conv_scratch(side, images):
    return [
        pltpu.VMEM((side + 2, side + 2, images, HALF), BF),
        pltpu.VMEM((TAPS * HALF, HALF), BF),
    ]


def place_vector(z, chip, core):
    return jnp.stack([z, chip, core]).astype(jnp.int32)


def with_place(kernel, grid, in_specs, out_specs, out_shape, flops, nbytes, scratch=(), vmem=24):
    return call(
        kernel,
        out_shape,
        flops,
        nbytes,
        vmem,
        grid_spec=pltpu.PrefetchScalarGridSpec(
            num_scalar_prefetch=1,
            grid=grid,
            in_specs=in_specs,
            out_specs=out_specs,
            scratch_shapes=list(scratch),
        ),
    )


def whole(shape):
    return pl.BlockSpec(shape, lambda s, p: (0,) * len(shape))


def rel_chip(slot, p):
    return p[0] ^ p[1] ^ slot


def fill_slots(p, refs, put):
    own, a, b, c, near, d, e = refs
    inner = (p[0] == 1) | (p[0] == 2)
    put(0, own)

    @pl.when(inner)
    def _():
        put(1, a)
        put(2, c)
        put(3, b)

    @pl.when(jnp.logical_not(inner))
    def _():
        put(1, near)
        put(2, d)
        put(3, e)


def put_columns(p, refs, sel, start, depth):
    width = sel.shape[3]

    def put(j, ref):
        sel[0, j, start : start + depth] = ref[:depth, :width]
        sel[1, j, start : start + depth] = ref[:depth, width:]

    fill_slots(p, refs, put)


def put_kernels(p, refs, conv):
    shard = conv.shape[0] // 4
    for i in range(4):
        start = pl.multiple_of((p[0] ^ i) * shard, 16)
        conv[pl.ds(start, shard), :] = refs[i][...]


def first_layer(place, x, piece, kernels, side):
    rows, width = x.shape
    images = rows // (side * side)
    shard = kernels[0].shape[0]

    def kernel(p, x_ref, own, a, c, d, *refs):
        sent, keep, hid, hid_t, slope, conv, sel, pad_ref, wide_ref = refs[4:]
        step = pl.program_id(0)
        inner = (p[0] == 1) | (p[0] == 2)

        @pl.when(step == 0)
        def _():
            def put_slot(j, ref):
                sel[0, j] = ref[:, :width]
                sel[1, j] = ref[:, width:]

            put_slot(0, own)
            put_slot(1, a)

            @pl.when(inner)
            def _():
                put_slot(2, c)

            @pl.when(jnp.logical_not(inner))
            def _():
                put_slot(2, d)

            put_kernels(p, refs[:4], conv)
            for h in range(width // HALF):
                lanes = slice(h * HALF, (h + 1) * HALF)

                def put(here, value, slant, lanes=lanes):
                    hid[here, lanes] = value
                    hid_t[lanes, here] = value.T
                    slope[here, lanes] = slant

                grid = x_ref[:, lanes].reshape(side, side, images, HALF)
                convolve(grid, conv.at[:, lanes], pad_ref, wide_ref, put)

        sent[0] = dot(hid[...], sel[1 - p[2], step]).astype(BF)
        keep[0] = dot(hid[...], sel[p[2], step]).astype(BF)

    mix_spec = pl.BlockSpec((1, rows, width), lambda s, p: (s, 0, 0))
    mix_shape = jax.ShapeDtypeStruct((3, rows, width), BF)
    return with_place(
        kernel,
        (3,),
        [whole((rows, width))] + [whole((width, 2 * width))] * 4 + [whole((shard, width))] * 4,
        (mix_spec, mix_spec)
        + (whole((rows, width)), whole((width, rows)), whole((rows, width)))
        + (whole((TAPS * GW, width)),),
        (
            mix_shape,
            mix_shape,
            jax.ShapeDtypeStruct((rows, width), BF),
            jax.ShapeDtypeStruct((width, rows), BF),
            jax.ShapeDtypeStruct((rows, width), F32),
            jax.ShapeDtypeStruct((TAPS * GW, width), BF),
        ),
        12 * rows * width * width + 2 * rows * HALF * width * TAPS,
        30 * rows * width,
        [pltpu.VMEM((2, 3, width, width), BF)] + conv_scratch(side, images),
        60,
    )(place, x, *piece, *kernels)


def last_slot(place, hidden, inner_piece, outer_piece):
    rows, width = hidden.shape

    def kernel(p, h_ref, b_ref, e_ref, sent, keep):
        inner = (p[0] == 1) | (p[0] == 2)
        for core in range(2):
            lanes = slice(core * width, (core + 1) * width)
            weights = jnp.where(inner, b_ref[:, lanes], e_ref[:, lanes])
            value = dot(h_ref[...], weights).astype(BF)

            @pl.when(p[2] == core)
            def _(value=value):
                keep[0] = value

            @pl.when(p[2] != core)
            def _(value=value):
                sent[0] = value

    shape = (1, rows, width)
    return with_place(
        kernel,
        (1,),
        [whole((rows, width))] + [whole((width, 2 * width))] * 2,
        (whole(shape), whole(shape)),
        (jax.ShapeDtypeStruct(shape, BF), jax.ShapeDtypeStruct(shape, BF)),
        4 * rows * width * width,
        12 * rows * width,
        (),
        24,
    )(place, hidden, inner_piece, outer_piece)


def sum_cores(place, keep, keep_last, other, other_last):
    _, rows, width = keep.shape
    cut = rows // 2

    def kernel(p, k_ref, kl_ref, o_ref, ol_ref, to_x, to_y, near, first_far, second_far):
        rel = pl.program_id(0)
        slot = rel_chip(rel, p)

        def both(here):
            early = add(k_ref[0, here, :], o_ref[0, here, :])
            late = add(kl_ref[0, here, :], ol_ref[0, here, :])
            return jnp.where(slot == 3, late, early)

        first, second = slice(0, cut), slice(cut, rows)

        @pl.when(rel == 0)
        def _():
            near[first, :] = both(first)
            near[second, :] = both(second)

        @pl.when(rel == 1)
        def _():
            to_x[0] = both(first).astype(BF)
            second_far[...] = both(second)

        @pl.when(rel == 2)
        def _():
            first_far[...] = both(first)
            to_y[0] = both(second).astype(BF)

        @pl.when(rel == 3)
        def _():
            to_x[1] = both(first).astype(BF)
            to_y[1] = both(second).astype(BF)

    early = pl.BlockSpec(
        (1, rows, width), lambda r, p: (jnp.minimum(rel_chip(r, p), 2), 0, 0)
    )
    last = whole((1, rows, width))
    pair, single = (2, cut, width), (cut, width)
    return with_place(
        kernel,
        (4,),
        [early, last, early, last],
        (whole(pair), whole(pair), whole((rows, width)), whole(single), whole(single)),
        (
            jax.ShapeDtypeStruct(pair, BF),
            jax.ShapeDtypeStruct(pair, BF),
            jax.ShapeDtypeStruct((rows, width), F32),
            jax.ShapeDtypeStruct(single, F32),
            jax.ShapeDtypeStruct(single, F32),
        ),
        0,
        24 * rows * width,
        (),
        32,
    )(place, keep, keep_last, other, other_last)


def next_layer(place, base, near_sum, first_x, second_y, first_y, second_x, kernels, from_inner, wide, side):
    rows, width = base.shape
    images = rows // (side * side)
    cut = rows // 2

    def kernel(p, b_ref, n_ref, fx, sy, fy, sx, *refs):
        below, g_ref = refs[4:6]
        x_ref, hid, slope, conv = refs[6:10]
        terms = refs[10:14]
        hid_t, pad_ref, wide_ref = refs[14:]
        step = pl.program_id(0)

        @pl.when(step == 0)
        def _():
            inner = (p[0] == 1) | (p[0] == 2)

            def put_shard(slot, start, value):
                there = pl.multiple_of((p[0] ^ slot) * shard + start, 16)
                conv[pl.ds(there, value.shape[0]), :] = value

            put_shard(0, 0, refs[0][...])

            @pl.when(inner)
            def _():
                for slot, ref in ((1, refs[1]), (3, refs[2]), (2, refs[3])):
                    put_shard(slot, 0, ref[...])

            @pl.when(jnp.logical_not(inner))
            def _():
                mid, end = width + shard, below.shape[0]
                put_shard(1, 0, below[width:mid, :width])
                put_shard(2, 0, below[width:mid, width:])
                put_shard(3, 0, below[mid:end, :width])
                put_shard(3, shard - (end - mid), below[mid:end, width:])

            near, far = slice(0, cut), slice(cut, rows)
            x_ref[near, :] = (
                add(b_ref[near, :]) + add(n_ref[near, :], fx[0], fy[...])
            ).astype(BF)
            x_ref[far, :] = (
                add(b_ref[far, :]) + add(n_ref[far, :], sy[0], sx[...])
            ).astype(BF)
            for h in range(width // HALF):
                lanes = slice(h * HALF, (h + 1) * HALF)

                def put(here, value, slant, lanes=lanes):
                    hid[here, lanes] = value
                    hid_t[lanes, here] = value.T
                    slope[here, lanes] = slant

                grid = x_ref[:, lanes].reshape(side, side, images, HALF)
                convolve(grid, conv.at[:, lanes], pad_ref, wide_ref, put)

        left = dot(hid_t[...], g_ref[0]).astype(BF)
        right = dot(hid_t[...], g_ref[1]).astype(BF)
        for i in range(4):

            @pl.when(step == i)
            def _(i=i):
                terms[i][:, :width] = left
                terms[i][:, width:] = right

    shard = kernels[0].shape[0]
    all_spec = whole((rows, width))
    return with_place(
        kernel,
        (4,),
        [
            all_spec,
            all_spec,
            whole((1, cut, width)),
            whole((1, cut, width)),
            whole((cut, width)),
            whole((cut, width)),
        ]
        + [whole(kernels[0].shape)] * 4
        + [whole(from_inner.shape)]
        + [pl.BlockSpec((2, rows, width), lambda i, p: (p[0] ^ i, 0, 0))],
        (all_spec, all_spec, all_spec, whole((TAPS * GW, width)))
        + (whole((width, 2 * width)),) * 4,
        (
            jax.ShapeDtypeStruct((rows, width), BF),
            jax.ShapeDtypeStruct((rows, width), BF),
            jax.ShapeDtypeStruct((rows, width), F32),
            jax.ShapeDtypeStruct((TAPS * GW, width), BF),
        )
        + (jax.ShapeDtypeStruct((width, 2 * width), BF),) * 4,
        16 * rows * width * width + 2 * rows * HALF * width * TAPS,
        32 * rows * width,
        [pltpu.VMEM((width, rows), BF)] + conv_scratch(side, images),
        60,
    )(place, base, near_sum, first_x, second_y, first_y, second_x, *kernels, from_inner, wide)


def output_gradient(place, wide, pieces, slope, conv, gradient, side):
    _, rows, width = wide.shape
    images = rows // (side * side)
    count = len(pieces)
    depth = width // count

    def kernel(p, s_ref, g_ref, *refs):
        c_ref, b_ref, gp_ref, o_ref, acc, sel, pad_ref, wide_ref = refs[7 * count :]
        step = pl.program_id(0)

        @pl.when(step == 0)
        def _():
            for k in range(count):
                put_columns(p, refs[7 * k : 7 * k + 7], sel, k * depth, depth)

        part = dot_nt(g_ref[0], sel[0, step]) + dot_nt(g_ref[1], sel[1, step])

        @pl.when(step == 0)
        def _():
            acc[...] = part

        @pl.when((step > 0) & (step < 3))
        def _():
            acc[...] += part

        @pl.when(step == 3)
        def _():
            gp_ref[...] = ((acc[...] + part) * s_ref[...]).astype(BF)
            for h in range(width // HALF):
                lanes = slice(h * HALF, (h + 1) * HALF)

                def put(here, field, lanes=lanes):
                    o_ref[here, lanes] = (b_ref[here, lanes].astype(F32) + field).astype(BF)

                grid = gp_ref[:, lanes].reshape(side, side, images, HALF)
                convolve_back(grid, c_ref.at[:, lanes], pad_ref, wide_ref, put)

    all_spec = whole((rows, width))
    return with_place(
        kernel,
        (4,),
        [all_spec, pl.BlockSpec((2, rows, width), lambda s, p: (p[0] ^ s, 0, 0))]
        + [whole((depth, 2 * width))] * (7 * count)
        + [whole((TAPS * GW, width)), all_spec],
        (all_spec, all_spec),
        (jax.ShapeDtypeStruct((rows, width), BF), jax.ShapeDtypeStruct((rows, width), BF)),
        16 * rows * width * width + 2 * rows * HALF * width * TAPS,
        32 * rows * width,
        [
            pltpu.VMEM((rows, width), F32),
            pltpu.VMEM((2, 4, width, width), BF),
            pltpu.VMEM((side + 2, side + 2, images, HALF), BF),
            pltpu.VMEM((HALF, TAPS * HALF), BF),
        ],
        60,
    )(place, slope, wide, *[a for piece in pieces for a in piece], conv, gradient)


def mix_columns(place, hidden, pieces):
    rows, width = hidden.shape
    count = len(pieces)
    depth = width // count

    def kernel(p, h_ref, *refs):
        sent, keep, sel = refs[7 * count :]
        step = pl.program_id(0)

        @pl.when(step == 0)
        def _():
            for k in range(count):
                put_columns(p, refs[7 * k : 7 * k + 7], sel, k * depth, depth)

        sent[0] = dot(h_ref[...], sel[1 - p[2], step]).astype(BF)
        keep[0] = dot(h_ref[...], sel[p[2], step]).astype(BF)

    mix_spec = pl.BlockSpec((1, rows, width), lambda s, p: (rel_chip(s, p), 0, 0))
    mix_shape = jax.ShapeDtypeStruct((4, rows, width), BF)
    return with_place(
        kernel,
        (4,),
        [whole(hidden.shape)] + [whole((depth, 2 * width))] * (7 * count),
        (mix_spec, mix_spec),
        (mix_shape, mix_shape),
        16 * rows * width * width,
        32 * rows * width,
        [pltpu.VMEM((2, 4, width, width), BF)],
        48,
    )(place, hidden, *[a for piece in pieces for a in piece])


def grad_pre(place, wides, piece, slope):
    rows, width = slope.shape
    count = len(wides)
    part_width = width // count

    def kernel(p, s_ref, *refs):
        g_refs = refs[: 2 * count]
        w_refs = refs[2 * count : 2 * count + 7]
        o_ref, sel, acc = refs[2 * count + 7 :]
        step = pl.program_id(0)

        @pl.when(step == 0)
        def _():
            put_columns(p, w_refs, sel, 0, width)

        part = None
        for k in range(count):
            lanes = slice(k * part_width, (k + 1) * part_width)
            for far in (0, 1):
                core = 1 - p[2] if far else p[2]
                term = dot_nt(g_refs[2 * k + far][0], sel[core, step, :, lanes])
                part = term if part is None else part + term

        @pl.when(step == 0)
        def _():
            acc[...] = part

        @pl.when((step > 0) & (step < 3))
        def _():
            acc[...] += part

        @pl.when(step == 3)
        def _():
            o_ref[...] = ((acc[...] + part) * s_ref[...]).astype(BF)

    return with_place(
        kernel,
        (4,),
        [whole((rows, width))]
        + [pl.BlockSpec((1, rows, part_width), lambda s, p: (rel_chip(s, p), 0, 0))] * (2 * count)
        + [whole((width, 2 * width))] * 7,
        whole((rows, width)),
        jax.ShapeDtypeStruct((rows, width), BF),
        16 * rows * width * width,
        32 * rows * width,
        [pltpu.VMEM((2, 4, width, width), BF), pltpu.VMEM((rows, width), F32)],
        60,
    )(place, slope, *[a for wide in wides for a in wide], *piece)


def mix_grad(place, hidden_t, wide, h, before=None):
    depth, rows = hidden_t.shape
    width = wide[0].shape[2]

    def kernel(p, h_ref, mine_ref, other_ref, *refs):
        term = refs[-1]
        mine = dot(h_ref[...], mine_ref[0]).astype(BF)
        rest = dot(h_ref[...], other_ref[0]).astype(BF)

        @pl.when(p[2] == 0)
        def _():
            term[0, :, :width] = mine
            term[0, :, width:] = rest

        @pl.when(p[2] == 1)
        def _():
            term[0, :, :width] = rest
            term[0, :, width:] = mine

    g_spec = pl.BlockSpec((1, rows, width), lambda c, p: (p[1] ^ c, 0, 0))
    specs = [whole((depth, rows)), g_spec, g_spec]
    args = [hidden_t, *wide]
    aliases = {}
    if before is not None:
        specs.append(pl.BlockSpec(memory_space=pl.ANY))
        args.append(before)
        aliases = {4: 0}
    return call(
        kernel,
        jax.ShapeDtypeStruct((4, depth, 4 * width), BF),
        16 * rows * depth * width,
        16 * (rows + depth) * width + 2 * rows * depth,
        60,
        grid_spec=pltpu.PrefetchScalarGridSpec(
            num_scalar_prefetch=1,
            grid=(4,),
            in_specs=specs,
            out_specs=pl.BlockSpec((1, depth, 2 * width), lambda c, p: (c, 0, h)),
        ),
        input_output_aliases=aliases,
    )(place, *args)


def conv_grad(place, x, gp, shard, side, relative):
    rows, width = x.shape
    images = rows // (side * side)

    def kernel(p, x_ref, gp_ref, o_ref, pad_ref, full_ref):
        mask = block_mask()
        for k in range(width // HALF):
            lanes = slice(k * HALF, (k + 1) * HALF)
            pad_field(x_ref[:, lanes].reshape(side, side, images, HALF), pad_ref)
            turned = gp_ref[:, lanes].T
            for tap in range(TAPS):
                a, b = tap // 3, tap % 3
                square = dot(turned, pad_ref[a : a + side, b : b + side].reshape(rows, HALF)).T
                square = jnp.where(mask, square, 0.0)
                slab = square[:GW]
                for q in range(1, HALF // GW):
                    slab = slab + square[q * GW : (q + 1) * GW]
                full_ref[tap * GW : (tap + 1) * GW, lanes] = slab.astype(BF)
        for plane in range(4):
            index = plane ^ p[0] if relative else plane
            o_ref[index] = full_ref[plane * shard : (plane + 1) * shard, :]

    return with_place(
        kernel,
        (1,),
        [whole((rows, width))] * 2,
        whole((4, shard, width)),
        jax.ShapeDtypeStruct((4, shard, width), BF),
        2 * rows * HALF * width * TAPS,
        rows * width * 4,
        [
            pltpu.VMEM((side + 2, side + 2, images, HALF), BF),
            pltpu.VMEM((4 * shard, width), BF),
        ],
    )(place, x, gp)


def conv_field(gp, w, gradient, side):
    rows, width = gp.shape
    images = rows // (side * side)

    def kernel(gp_ref, w_ref, g_ref, o_ref, pad_ref, wide_ref):
        def put(here, field):
            o_ref[here, :] = (g_ref[here, :].astype(F32) + field).astype(BF)

        grid = gp_ref[...].reshape(side, side, images, HALF)
        convolve_back(grid, w_ref, pad_ref, wide_ref, put)

    half_spec = pl.BlockSpec((rows, HALF), lambda h: (0, h))
    return call(
        kernel,
        jax.ShapeDtypeStruct((rows, width), BF),
        2 * rows * HALF * width * TAPS,
        rows * width * 6,
        grid=(width // HALF,),
        in_specs=[half_spec, pl.BlockSpec((TAPS * GW, HALF), lambda h: (0, h)), half_spec],
        out_specs=half_spec,
        scratch_shapes=[
            pltpu.VMEM((side + 2, side + 2, images, HALF), BF),
            pltpu.VMEM((HALF, TAPS * HALF), BF),
        ],
    )(gp, w, gradient)


def finish(place, scale, last, first, convs, convs_last, mix_shape, conv_shape):
    layers, depth, width = mix_shape
    _, shard, channels = conv_shape

    def kernel(p, own, near, inner, first_ref, *refs):
        del p
        mix_ref, conv_ref = refs[-2:]
        mix_ref[1] = add(own[...], near[...], inner[...]) * scale
        for half in range(2):
            for core in range(2):
                there = core * 2 * HALF + half * HALF
                here = half * 2 * HALF + core * HALF
                mix_ref[0, :, there : there + HALF] = (
                    first_ref[0, :, here : here + HALF].astype(F32) * scale
                )
        for layer in range(2):
            four = refs[4 * layer : 4 * layer + 4]
            conv_ref[layer] = add(four[0][0], *[ref[...] for ref in four[1:]]) * scale

    convs_spec = [whole((1, shard, channels))] + [whole((shard, channels))] * 3
    return with_place(
        kernel,
        (1,),
        [whole((depth, width))] * 3 + [whole((1, depth, width))] + convs_spec * 2,
        (whole(mix_shape), whole(conv_shape)),
        (jax.ShapeDtypeStruct(mix_shape, F32), jax.ShapeDtypeStruct(conv_shape, F32)),
        0,
        12 * depth * width,
        (),
        60,
    )(place, *last, first, *convs, *convs_last)


def after(value, *others):
    return lax.optimization_barrier((value, *others))[0]


class Clock:
    def __init__(self, token):
        self.token = token

    def gate(self, value):
        return lax.optimization_barrier((value, self.token))[0]

    def close(self, *values):
        self.token, *values = lax.optimization_barrier((self.token, *values))
        return values


def permute_dp(value, pairs):
    return lax.ppermute(value, "dp", pairs)


def permute_group(value, pairs):
    return lax.ppermute(value, "group", pairs)


def add(*terms):
    total = terms[0].astype(F32)
    for term in terms[1:]:
        total = total + term.astype(F32)
    return total


def gather_outer(own):
    return permute_dp(own, OUTER_INNER)


def gather_inner(own):
    return permute_dp(own, INNER)


def gather_second(a, b):
    return permute_dp(a, INNER), permute_dp(b, OUTWARD)


def gather_third(c):
    return permute_dp(c, OUTWARD)


def scatter_direct(parts):
    return [permute_dp(parts[i], [(j, j ^ i) for j in range(4)]) for i in (1, 2, 3)]


def plane_first(own):
    cut = own.shape[0] // 2
    return permute_group(own[:cut], ACROSS_X), permute_group(own[cut:], ACROSS_Y)


def plane_second(own, first_x, second_y):
    cut = own.shape[0] // 2
    return (
        permute_group(jnp.stack([own[:cut], first_x]), ACROSS_Y),
        permute_group(jnp.stack([own[cut:], second_y]), ACROSS_X),
    )


def plane_join(own, first_x, second_y, first_y, second_x):
    return jnp.stack(
        [
            own,
            jnp.concatenate([first_x, second_x[0]]),
            jnp.concatenate([first_y[0], second_y]),
            jnp.concatenate([first_y[1], second_x[1]]),
        ]
    )


def across_cores(value):
    return permute_group(value, ACROSS_CORE)


def sum_last(base, keep, other, first_x, second_y, first_y, second_x):
    cut = base.shape[0] // 2
    return jnp.concatenate(
        [
            add(base[:cut]) + add(keep[0, :cut], other[0, :cut], first_x[0], first_y),
            add(base[cut:]) + add(keep[0, cut:], other[0, cut:], second_y[0], second_x),
        ]
    ).astype(BF)


def sum_first(keep, other):
    rows = keep.shape[1]
    cut = rows // 2
    first = [add(keep[c, :cut], other[c, :cut]).astype(BF) for c in (1, 3)]
    second = [add(keep[c, cut:], other[c, cut:]).astype(BF) for c in (2, 3)]
    return (
        permute_group(jnp.stack(first), ACROSS_X),
        permute_group(jnp.stack(second), ACROSS_Y),
    )


def sum_second(keep, other, first_x, second_y):
    cut = keep.shape[1] // 2
    return (
        permute_group(add(keep[2, :cut], other[2, :cut], first_x[1]).astype(BF), ACROSS_Y),
        permute_group(add(keep[1, cut:], other[1, cut:], second_y[1]).astype(BF), ACROSS_X),
    )


def staged(images, cotangent, conv_weight, mix_weight):
    batch, side, _, width = images.shape
    shard = conv_weight.shape[1]
    rows = batch * side * side
    scale = 1.0 / math.sqrt(rows * lax.axis_size("dp"))
    z = lax.axis_index("dp")
    group = lax.axis_index("group")
    place = place_vector(z, group // 2, group % 2)
    clock = Clock(z)
    gate, close = clock.gate, clock.close

    def to_rows(field):
        return field.transpose(1, 2, 0, 3).reshape(rows, width)

    def from_rows(flat):
        return flat.reshape(side, side, batch, width).transpose(2, 0, 1, 3)

    def half(flat, h):
        return flat[:, h * HALF : (h + 1) * HALF]

    own0, own1 = mix_weight[0], mix_weight[1]
    a0, b0 = gather_outer(own0), gather_inner(own0)
    kernels0 = [conv_weight[0], *scatter_direct([conv_weight[0]] * 4)]
    x0 = to_rows(images)
    g2 = to_rows(cotangent)
    a0, b0, x0, g2, *kernels0 = close(a0, b0, x0, g2, *kernels0)

    wide2 = lax.all_gather(gate(g2), "group", axis=0)
    c0, d0 = gather_second(a0, b0)
    shard1 = gate(conv_weight[1])
    ka, kb = permute_dp(shard1, INWARD), gather_inner(shard1)
    a1 = permute_dp(gate(own1), INWARD)
    c0, d0, ka, kb, a1 = close(c0, d0, ka, kb, a1)

    e0 = gather_third(c0)
    kc = gather_inner(ka)
    b1 = gather_inner(after(own1, kc))
    tall = (shard // 2 + 15) // 16 * 16
    pairs = ((conv_weight[1], kb), (kc[:tall], kc[shard - tall :]))
    below = [jnp.concatenate(pair, axis=1) for pair in pairs]
    from_inner = jnp.concatenate([own1, *below])
    sent, keep, hidden0, hidden0_t, slope0, conv0 = first_layer(
        place, x0, (own0, a0, c0, d0), kernels0, side
    )
    e0, b1, kc, from_inner, sent, keep, hidden0, hidden0_t, slope0, conv0 = close(
        e0, b1, kc, from_inner, sent, keep, hidden0, hidden0_t, slope0, conv0
    )
    p0 = (own0, a0, b0, c0, a0, d0, e0)

    near1, c1 = gather_third(from_inner), gather_inner(a1)
    other = across_cores(sent)
    sent_last, keep_last = last_slot(place, hidden0, b0, e0)
    other_last = across_cores(sent_last)
    to_x, to_y, near, first_far, second_far = sum_cores(place, keep, keep_last, other, other_last)
    sx, sy = permute_group(to_x, ACROSS_X), permute_group(to_y, ACROSS_Y)
    d1, e1 = gather_third(after(b1, near1, to_x)), gather_third(after(c1, near1, to_x))
    ty = permute_group(add(first_far, sx[1]).astype(BF), ACROSS_Y)
    tx = permute_group(add(second_far, sy[1]).astype(BF), ACROSS_X)

    x1, hidden1, slope1, conv1, *m1 = next_layer(
        place, x0, near, sx, sy, ty, tx, (conv_weight[1], ka, kb, kc), near1, wide2, side
    )
    first_in, second_in = permute_dp(after(m1[3], d1), INWARD), permute_dp(m1[2], INWARD)
    across = permute_dp(add(m1[2], first_in).astype(BF), INNER)
    p1 = (own1, a1, b1, c1, near1, d1, e1)

    gp1, g1 = output_gradient(place, wide2, [p1], after(slope1, first_in), conv1, g2, side)
    ax, ay = plane_first(g1)
    gp1, g1, ax, ay, across, second_in = close(gp1, g1, ax, ay, across, second_in)
    near_sum = permute_dp(add(m1[1], across).astype(BF), OUTER_INNER)
    inner_sum = permute_dp(add(m1[3], second_in).astype(BF), INNER)
    own_a, own_b = half(g1, 0), half(g1, 1)
    ayy, axx = plane_second(own_a, half(ax, 0), half(ay, 0))
    byy, bxx = plane_second(own_b, half(ax, 1), half(ay, 1))
    terms1 = conv_grad(place, x1, gp1, shard, side, True)
    ayy, axx, terms1 = close(ayy, axx, terms1)
    moved = scatter_direct(terms1)
    mine_a = plane_join(own_a, half(ax, 0), half(ay, 0), ayy, axx)
    wide_a = (mine_a, across_cores(mine_a))
    m0 = mix_grad(place, hidden0_t, wide_a, 0)
    byy, bxx, near_sum, inner_sum = close(byy, bxx, near_sum, inner_sum)
    mine_b = plane_join(own_b, half(ax, 1), half(ay, 1), byy, bxx)
    wide_b = (mine_b, across_cores(mine_b))
    m0 = mix_grad(place, hidden0_t, wide_b, 1, m0)
    m0, *moved = close(m0, *moved)
    first = lax.psum_scatter(m0, "dp", scatter_dimension=0, tiled=True)
    last = (m1[0], near_sum, inner_sum)
    conv_last = [terms1, *moved]

    gp0 = grad_pre(place, [wide_a, wide_b], p0, slope0)
    terms0 = conv_grad(place, x0, gp0, shard, side, True)
    gp0, terms0 = close(gp0, terms0)
    cs = scatter_direct(terms0)

    sent, keep = mix_columns(place, gate(hidden1), [p1])
    other = across_cores(sent)
    keep, other = close(keep, other)
    sx, sy = sum_first(keep, other)
    g0 = conv_field(gp0, conv0, g1, side)
    sx, sy, g0 = close(sx, sy, g0)
    ty, tx = sum_second(keep, other, sx, sy)
    features = from_rows(sum_last(x1, keep, other, sx, sy, ty, tx))
    grad_images = from_rows(g0)
    grad_mix, grad_conv = finish(
        place, scale, last, first, [terms0, *cs], conv_last, mix_weight.shape, conv_weight.shape
    )
    return features, grad_images, grad_conv, grad_mix


def make_patches(field):
    side_cells = field.shape[1]
    padded = jnp.pad(field, ((0, 0), (1, 1), (1, 1), (0, 0)))
    tap_list = [
        padded[:, row_shift : row_shift + side_cells, col_shift : col_shift + side_cells, :]
        for row_shift in range(3)
        for col_shift in range(3)
    ]
    return jnp.stack(tap_list, axis=3).reshape(-1, 9, field.shape[3])


def fold_patches(pieces, batch_size, side_cells):
    pieces = pieces.reshape(batch_size, side_cells, side_cells, 9, pieces.shape[2])
    summed = jnp.zeros((batch_size, side_cells + 2, side_cells + 2, pieces.shape[4]), F32)
    for tap_index in range(9):
        row_shift = tap_index // 3
        col_shift = tap_index % 3
        summed = summed + jnp.pad(
            pieces[:, :, :, tap_index, :],
            ((0, 0), (row_shift, 2 - row_shift), (col_shift, 2 - col_shift), (0, 0)),
        )
    return summed[:, 1 : side_cells + 1, 1 : side_cells + 1, :]


def silu_slope(value):
    sigmoid_v = jax.nn.sigmoid(value)
    return sigmoid_v * (1.0 + value * (1.0 - sigmoid_v))


def general(images, cotangent, conv_weight, mix_weight):
    batch_size, side_cells, _, local_width = images.shape
    local_groups = local_width // GW
    row_count = batch_size * side_cells * side_cells
    layer_count = conv_weight.shape[0]
    grad_scale = 1.0 / math.sqrt(row_count * lax.axis_size("dp"))
    fetched = [
        (
            lax.all_gather(conv_weight[layer], "dp", axis=0, tiled=True),
            lax.all_gather(mix_weight[layer], "dp", axis=1, tiled=True),
        )
        for layer in range(layer_count)
    ]
    current = images
    saved = []
    for layer in range(layer_count):
        conv_full, mix_full = fetched[layer]
        tap_weights = conv_full.reshape(9 * GW, local_groups, GW).transpose(1, 0, 2)
        flat = make_patches(current).reshape(row_count, 9, local_groups, GW)
        patches = flat.transpose(0, 2, 1, 3).reshape(row_count, local_groups, 9 * GW)
        pre_act = jnp.einsum(
            "pgk,gko->pgo", patches, tap_weights, preferred_element_type=F32
        ).reshape(row_count, local_width)
        hidden = jax.nn.silu(pre_act).astype(BF)
        mixed = lax.psum_scatter(
            jnp.dot(hidden, mix_full, preferred_element_type=F32).astype(BF),
            "group",
            scatter_dimension=1,
            tiled=True,
        ).astype(F32)
        saved.append((patches, pre_act, hidden, tap_weights, mix_full))
        current = (
            (current.reshape(row_count, local_width).astype(F32) + mixed)
            .astype(BF)
            .reshape(images.shape)
        )
    gradient = cotangent
    conv_grads = []
    mix_grads = []
    for layer in reversed(range(layer_count)):
        patches, pre_act, hidden, tap_weights, mix_full = saved[layer]
        flat_grad = gradient.reshape(row_count, local_width)
        grad_wide = lax.all_gather(flat_grad, "group", axis=1, tiled=True)
        mix_term = lax.dot_general(
            hidden, grad_wide, (((0,), (0,)), ((), ())), preferred_element_type=F32
        )
        grad_hidden = dot_nt(grad_wide, mix_full)
        grad_pre = (
            (grad_hidden * silu_slope(pre_act)).astype(BF).reshape(row_count, local_groups, GW)
        )
        conv_term = jnp.einsum("pgk,pgo->gko", patches, grad_pre, preferred_element_type=F32)
        conv_term = conv_term.transpose(1, 0, 2).reshape(9 * GW, local_width)
        patch_grad = jnp.einsum("pgo,gko->pgk", grad_pre, tap_weights, preferred_element_type=F32)
        patch_grad = (
            patch_grad.reshape(row_count, local_groups, 9, GW)
            .transpose(0, 2, 1, 3)
            .reshape(row_count, 9, local_width)
        )
        field_grad = fold_patches(patch_grad, batch_size, side_cells)
        conv_summed, mix_summed = (
            lax.psum_scatter(
                conv_term.astype(BF), "dp", scatter_dimension=0, tiled=True
            ).astype(F32),
            lax.psum_scatter(
                mix_term.astype(BF), "dp", scatter_dimension=1, tiled=True
            ).astype(F32),
        )
        conv_grads.insert(0, conv_summed * grad_scale)
        mix_grads.insert(0, mix_summed * grad_scale)
        gradient = (gradient.astype(F32) + field_grad).astype(BF)
    return (current, gradient, jnp.stack(conv_grads), jnp.stack(mix_grads))


def solution(mesh):
    fits = mesh.shape["dp"] == 4 and mesh.shape["group"] == 8
    return jax.shard_map(
        staged if fits else general,
        mesh=mesh,
        in_specs=(
            P("dp", None, None, "group"),
            P("dp", None, None, "group"),
            P(None, "dp", "group"),
            P(None, "group", "dp"),
        ),
        out_specs=(
            P("dp", None, None, "group"),
            P("dp", None, None, "group"),
            P(None, "dp", "group"),
            P(None, "group", "dp"),
        ),
        check_vma=False,
    )
```

```python
import functools
import math

import jax
import jax.numpy as jnp
from jax import lax
from jax.experimental import pallas as pl
from jax.experimental.pallas import tpu as pltpu
from jax.sharding import PartitionSpec as P

GW = 64
TAPS = 9
HALF = 256
BF = jnp.bfloat16
F32 = jnp.float32
MIB = 1024 * 1024

OUTER_INNER = [(0, 1), (1, 0), (2, 3), (3, 2)]
INNER = [(1, 2), (2, 1)]
OUTWARD = [(1, 0), (2, 3)]
INWARD = [(0, 1), (3, 2)]
ACROSS_CORE = [(i, i ^ 1) for i in range(8)]
ACROSS_X = [(i, i ^ 2) for i in range(8)]
ACROSS_Y = [(i, i ^ 4) for i in range(8)]


def dot(a, b):
    return jnp.dot(a, b, preferred_element_type=F32)


def dot_nt(a, b):
    return lax.dot_general(a, b, (((1,), (1,)), ((), ())), preferred_element_type=F32)


def call(kernel, out_shape, flops, nbytes, vmem=24, **kw):
    return pl.pallas_call(
        kernel,
        out_shape=out_shape,
        compiler_params=pltpu.CompilerParams(vmem_limit_bytes=vmem * MIB),
        cost_estimate=pl.CostEstimate(flops=flops, bytes_accessed=nbytes, transcendentals=0),
        **kw,
    )


def block_mask():
    rows = lax.broadcasted_iota(jnp.int32, (HALF, HALF), 0) // GW
    cols = lax.broadcasted_iota(jnp.int32, (HALF, HALF), 1) // GW
    return rows == cols


def spread_taps(w_ref, wide_ref, by_rows):
    mask = block_mask()
    for tap in range(TAPS):
        slab = w_ref[tap * GW : (tap + 1) * GW, :]
        square = jnp.concatenate([slab] * (HALF // GW), axis=0)
        square = jnp.where(mask, square, jnp.zeros_like(square))
        if by_rows:
            wide_ref[tap * HALF : (tap + 1) * HALF, :] = square
        else:
            wide_ref[:, tap * HALF : (tap + 1) * HALF] = square


def pad_field(value, pad_ref):
    side = value.shape[0]
    pad_ref[...] = jnp.zeros_like(pad_ref)
    pad_ref[1 : side + 1, 1 : side + 1] = value


STRIP = 2


def strips(pad_ref, flipped):
    side, images = pad_ref.shape[0] - 2, pad_ref.shape[2]
    rows = STRIP * side * images
    for part in range(side // STRIP):
        top = part * STRIP
        taps = [(2 - a, 2 - b) if flipped else (a, b) for a in range(3) for b in range(3)]
        patches = jnp.concatenate(
            [
                pad_ref[top + a : top + a + STRIP, b : b + side].reshape(rows, HALF)
                for a, b in taps
            ],
            axis=1,
        )
        yield slice(part * rows, (part + 1) * rows), patches


def convolve(x, w_ref, pad_ref, wide_ref, put):
    pad_field(x, pad_ref)
    spread_taps(w_ref, wide_ref, True)
    for here, patches in strips(pad_ref, False):
        pre = dot(patches, wide_ref[...])
        sig = jax.nn.sigmoid(pre)
        put(here, (pre * sig).astype(BF), sig * (1.0 + pre * (1.0 - sig)))


def convolve_back(gp, w_ref, pad_ref, wide_ref, put):
    pad_field(gp, pad_ref)
    spread_taps(w_ref, wide_ref, False)
    for here, patches in strips(pad_ref, True):
        put(here, dot_nt(patches, wide_ref[...]))


def conv_scratch(side, images):
    return [
        pltpu.VMEM((side + 2, side + 2, images, HALF), BF),
        pltpu.VMEM((TAPS * HALF, HALF), BF),
    ]


def place_vector(z, chip, core):
    return jnp.stack([z, chip, core]).astype(jnp.int32)


def with_place(kernel, grid, in_specs, out_specs, out_shape, flops, nbytes, scratch=(), vmem=24):
    return call(
        kernel,
        out_shape,
        flops,
        nbytes,
        vmem,
        grid_spec=pltpu.PrefetchScalarGridSpec(
            num_scalar_prefetch=1,
            grid=grid,
            in_specs=in_specs,
            out_specs=out_specs,
            scratch_shapes=list(scratch),
        ),
    )


def whole(shape):
    return pl.BlockSpec(shape, lambda s, p: (0,) * len(shape))


def rel_chip(slot, p):
    return p[0] ^ p[1] ^ slot


def fill_slots(p, refs, put):
    own, a, b, c, d, e = refs
    inner = (p[0] == 1) | (p[0] == 2)
    put(0, own)
    put(1, a)

    @pl.when(inner)
    def _():
        put(2, c)
        put(3, b)

    @pl.when(jnp.logical_not(inner))
    def _():
        put(2, d)
        put(3, e)


def put_columns(p, refs, sel, start, depth):
    width = sel.shape[3]

    def put(j, ref):
        sel[0, j, start : start + depth] = ref[:depth, :width]
        sel[1, j, start : start + depth] = ref[:depth, width:]

    fill_slots(p, refs, put)


def put_kernels(p, refs, conv, depth, tall):
    width = conv.shape[1]
    shard = conv.shape[0] // 4

    def put(j, ref):
        put_shard(p, j, conv, ref[depth : depth + tall, :width], 0)
        put_shard(p, j, conv, ref[depth : depth + tall, width:], shard - tall)

    fill_slots(p, refs, put)


def put_shard(p, slot, conv, value, offset):
    shard = conv.shape[0] // 4
    start = pl.multiple_of((p[0] ^ slot) * shard + offset, 16)
    conv[pl.ds(start, value.shape[0]), :] = value


def first_layer(place, x, piece, far, side):
    rows, width = x.shape
    images = rows // (side * side)
    tall = piece[0].shape[0] - width

    def kernel(p, x_ref, own, a, b, c, d, far_ref, *refs):
        sent, keep, hid, hid_t, slope, conv, sel, pad_ref, wide_ref = refs
        step = pl.program_id(0)
        inner = (p[0] == 1) | (p[0] == 2)

        @pl.when(step == 0)
        def _():
            shard = conv.shape[0] // 4

            def put_slot(j, ref):
                if j < 3:
                    sel[0, j] = ref[:width, :width]
                    sel[1, j] = ref[:width, width:]
                put_shard(p, j, conv, ref[width:, :width], 0)
                put_shard(p, j, conv, ref[width:, width:], shard - tall)

            put_slot(0, own)
            put_slot(1, a)

            @pl.when(inner)
            def _():
                put_slot(2, c)
                put_slot(3, b)

            @pl.when(jnp.logical_not(inner))
            def _():
                put_slot(2, d)
                put_shard(p, 3, conv, far_ref[...], 0)

            for h in range(width // HALF):
                lanes = slice(h * HALF, (h + 1) * HALF)

                def put(here, value, slant, lanes=lanes):
                    hid[here, lanes] = value
                    hid_t[lanes, here] = value.T
                    slope[here, lanes] = slant

                grid = x_ref[:, lanes].reshape(side, side, images, HALF)
                convolve(grid, conv.at[:, lanes], pad_ref, wide_ref, put)

        sent[0] = dot(hid[...], sel[1 - p[2], step]).astype(BF)
        keep[0] = dot(hid[...], sel[p[2], step]).astype(BF)

    mix_spec = pl.BlockSpec((1, rows, width), lambda s, p: (s, 0, 0))
    mix_shape = jax.ShapeDtypeStruct((3, rows, width), BF)
    return with_place(
        kernel,
        (3,),
        [whole((rows, width))] + [whole(piece[0].shape)] * 5 + [whole(far.shape)],
        (mix_spec, mix_spec)
        + (whole((rows, width)), whole((width, rows)), whole((rows, width)))
        + (whole((TAPS * GW, width)),),
        (
            mix_shape,
            mix_shape,
            jax.ShapeDtypeStruct((rows, width), BF),
            jax.ShapeDtypeStruct((width, rows), BF),
            jax.ShapeDtypeStruct((rows, width), F32),
            jax.ShapeDtypeStruct((TAPS * GW, width), BF),
        ),
        12 * rows * width * width + 2 * rows * HALF * width * TAPS,
        30 * rows * width,
        [pltpu.VMEM((2, 3, width, width), BF)] + conv_scratch(side, images),
        60,
    )(place, x, *piece, far)


def last_slot(place, hidden, inner_piece, outer_piece):
    rows, width = hidden.shape

    def kernel(p, h_ref, b_ref, e_ref, sent, keep):
        inner = (p[0] == 1) | (p[0] == 2)
        for core in range(2):
            lanes = slice(core * width, (core + 1) * width)
            weights = jnp.where(inner, b_ref[:, lanes], e_ref[:, lanes])
            value = dot(h_ref[...], weights).astype(BF)

            @pl.when(p[2] == core)
            def _(value=value):
                keep[0] = value

            @pl.when(p[2] != core)
            def _(value=value):
                sent[0] = value

    shape = (1, rows, width)
    return with_place(
        kernel,
        (1,),
        [whole((rows, width))] + [whole((width, 2 * width))] * 2,
        (whole(shape), whole(shape)),
        (jax.ShapeDtypeStruct(shape, BF), jax.ShapeDtypeStruct(shape, BF)),
        4 * rows * width * width,
        12 * rows * width,
        (),
        24,
    )(place, hidden, inner_piece, outer_piece)


def sum_cores(place, keep, keep_last, other, other_last):
    _, rows, width = keep.shape
    cut = rows // 2

    def kernel(p, k_ref, kl_ref, o_ref, ol_ref, to_x, to_y, near, first_far, second_far):
        rel = pl.program_id(0)
        slot = rel_chip(rel, p)

        def both(here):
            early = add(k_ref[0, here, :], o_ref[0, here, :])
            late = add(kl_ref[0, here, :], ol_ref[0, here, :])
            return jnp.where(slot == 3, late, early)

        first, second = slice(0, cut), slice(cut, rows)

        @pl.when(rel == 0)
        def _():
            near[first, :] = both(first)
            near[second, :] = both(second)

        @pl.when(rel == 1)
        def _():
            to_x[0] = both(first).astype(BF)
            second_far[...] = both(second)

        @pl.when(rel == 2)
        def _():
            first_far[...] = both(first)
            to_y[0] = both(second).astype(BF)

        @pl.when(rel == 3)
        def _():
            to_x[1] = both(first).astype(BF)
            to_y[1] = both(second).astype(BF)

    early = pl.BlockSpec(
        (1, rows, width), lambda r, p: (jnp.minimum(rel_chip(r, p), 2), 0, 0)
    )
    last = whole((1, rows, width))
    pair, single = (2, cut, width), (cut, width)
    return with_place(
        kernel,
        (4,),
        [early, last, early, last],
        (whole(pair), whole(pair), whole((rows, width)), whole(single), whole(single)),
        (
            jax.ShapeDtypeStruct(pair, BF),
            jax.ShapeDtypeStruct(pair, BF),
            jax.ShapeDtypeStruct((rows, width), F32),
            jax.ShapeDtypeStruct(single, F32),
            jax.ShapeDtypeStruct(single, F32),
        ),
        0,
        24 * rows * width,
        (),
        32,
    )(place, keep, keep_last, other, other_last)


def next_layer(place, base, near_sum, first_x, second_y, first_y, second_x, piece, start, wide, side):
    rows, width = base.shape
    images = rows // (side * side)
    cut = rows // 2

    def kernel(p, b_ref, n_ref, fx, sy, fy, sx, *refs):
        g_ref = refs[6]
        x_ref, hid, slope, conv, term = refs[7:12]
        hid_t, pad_ref, wide_ref = refs[12:]
        step = pl.program_id(0)

        @pl.when(step == 0)
        def _():
            put_kernels(p, refs[:6], conv, 0, tall)
            near, far = slice(0, cut), slice(cut, rows)
            x_ref[near, :] = (
                add(b_ref[near, :]) + add(n_ref[near, :], fx[0], fy[...])
            ).astype(BF)
            x_ref[far, :] = (
                add(b_ref[far, :]) + add(n_ref[far, :], sy[0], sx[...])
            ).astype(BF)
            for h in range(width // HALF):
                lanes = slice(h * HALF, (h + 1) * HALF)

                def put(here, value, slant, lanes=lanes):
                    hid[here, lanes] = value
                    hid_t[lanes, here] = value.T
                    slope[here, lanes] = slant

                grid = x_ref[:, lanes].reshape(side, side, images, HALF)
                convolve(grid, conv.at[:, lanes], pad_ref, wide_ref, put)

        term[0, :, :width] = dot(hid_t[...], g_ref[0]).astype(BF)
        term[0, :, width:] = dot(hid_t[...], g_ref[1]).astype(BF)

    all_spec = whole((rows, width))
    tall = piece[0].shape[0] - start
    block = math.gcd(start, 128)
    return with_place(
        kernel,
        (4,),
        [
            all_spec,
            all_spec,
            whole((1, cut, width)),
            whole((1, cut, width)),
            whole((cut, width)),
            whole((cut, width)),
        ]
        + [pl.BlockSpec((block, 2 * width), lambda s, p: (start // block, 0))] * 6
        + [pl.BlockSpec((2, rows, width), lambda c, p: (c, 0, 0))],
        (
            all_spec,
            all_spec,
            all_spec,
            whole((TAPS * GW, width)),
            pl.BlockSpec((1, width, 2 * width), lambda c, p: (c, 0, 0)),
        ),
        (
            jax.ShapeDtypeStruct((rows, width), BF),
            jax.ShapeDtypeStruct((rows, width), BF),
            jax.ShapeDtypeStruct((rows, width), F32),
            jax.ShapeDtypeStruct((TAPS * GW, width), BF),
            jax.ShapeDtypeStruct((4, width, 2 * width), BF),
        ),
        16 * rows * width * width + 2 * rows * HALF * width * TAPS,
        32 * rows * width,
        [pltpu.VMEM((width, rows), BF)] + conv_scratch(side, images),
        60,
    )(place, base, near_sum, first_x, second_y, first_y, second_x, *piece, wide)


def output_gradient(place, wide, pieces, slope, conv, gradient, side):
    _, rows, width = wide.shape
    images = rows // (side * side)
    count = len(pieces)
    depth = width // count

    def kernel(p, s_ref, g_ref, *refs):
        c_ref, b_ref, gp_ref, o_ref, acc, sel, pad_ref, wide_ref = refs[6 * count :]
        step = pl.program_id(0)

        @pl.when(step == 0)
        def _():
            for k in range(count):
                put_columns(p, refs[6 * k : 6 * k + 6], sel, k * depth, depth)

        part = dot_nt(g_ref[0], sel[0, step]) + dot_nt(g_ref[1], sel[1, step])

        @pl.when(step == 0)
        def _():
            acc[...] = part

        @pl.when((step > 0) & (step < 3))
        def _():
            acc[...] += part

        @pl.when(step == 3)
        def _():
            gp_ref[...] = ((acc[...] + part) * s_ref[...]).astype(BF)
            for h in range(width // HALF):
                lanes = slice(h * HALF, (h + 1) * HALF)

                def put(here, field, lanes=lanes):
                    o_ref[here, lanes] = (b_ref[here, lanes].astype(F32) + field).astype(BF)

                grid = gp_ref[:, lanes].reshape(side, side, images, HALF)
                convolve_back(grid, c_ref.at[:, lanes], pad_ref, wide_ref, put)

    all_spec = whole((rows, width))
    return with_place(
        kernel,
        (4,),
        [all_spec, pl.BlockSpec((2, rows, width), lambda s, p: (p[0] ^ s, 0, 0))]
        + [whole((depth, 2 * width))] * (6 * count)
        + [whole((TAPS * GW, width)), all_spec],
        (all_spec, all_spec),
        (jax.ShapeDtypeStruct((rows, width), BF), jax.ShapeDtypeStruct((rows, width), BF)),
        16 * rows * width * width + 2 * rows * HALF * width * TAPS,
        32 * rows * width,
        [
            pltpu.VMEM((rows, width), F32),
            pltpu.VMEM((2, 4, width, width), BF),
            pltpu.VMEM((side + 2, side + 2, images, HALF), BF),
            pltpu.VMEM((HALF, TAPS * HALF), BF),
        ],
        60,
    )(place, slope, wide, *[a for piece in pieces for a in piece], conv, gradient)


def mix_columns(place, hidden, pieces):
    rows, width = hidden.shape
    count = len(pieces)
    depth = width // count

    def kernel(p, h_ref, *refs):
        sent, keep, sel = refs[6 * count :]
        step = pl.program_id(0)

        @pl.when(step == 0)
        def _():
            for k in range(count):
                put_columns(p, refs[6 * k : 6 * k + 6], sel, k * depth, depth)

        sent[0] = dot(h_ref[...], sel[1 - p[2], step]).astype(BF)
        keep[0] = dot(h_ref[...], sel[p[2], step]).astype(BF)

    mix_spec = pl.BlockSpec((1, rows, width), lambda s, p: (rel_chip(s, p), 0, 0))
    mix_shape = jax.ShapeDtypeStruct((4, rows, width), BF)
    return with_place(
        kernel,
        (4,),
        [whole(hidden.shape)] + [whole((depth, 2 * width))] * (6 * count),
        (mix_spec, mix_spec),
        (mix_shape, mix_shape),
        16 * rows * width * width,
        32 * rows * width,
        [pltpu.VMEM((2, 4, width, width), BF)],
        48,
    )(place, hidden, *[a for piece in pieces for a in piece])


def grad_pre(place, wide, piece, slope):
    rows, width = slope.shape

    def kernel(p, s_ref, mine_ref, other_ref, *refs):
        o_ref, sel, acc = refs[6:]
        step = pl.program_id(0)

        @pl.when(step == 0)
        def _():
            put_columns(p, refs[:6], sel, 0, width)

        part = dot_nt(mine_ref[0], sel[p[2], step]) + dot_nt(other_ref[0], sel[1 - p[2], step])

        @pl.when(step == 0)
        def _():
            acc[...] = part

        @pl.when((step > 0) & (step < 3))
        def _():
            acc[...] += part

        @pl.when(step == 3)
        def _():
            o_ref[...] = ((acc[...] + part) * s_ref[...]).astype(BF)

    return with_place(
        kernel,
        (4,),
        [whole((rows, width))]
        + [pl.BlockSpec((1, rows, width), lambda s, p: (rel_chip(s, p), 0, 0))] * 2
        + [whole((width, 2 * width))] * 6,
        whole((rows, width)),
        jax.ShapeDtypeStruct((rows, width), BF),
        16 * rows * width * width,
        32 * rows * width,
        [pltpu.VMEM((2, 4, width, width), BF), pltpu.VMEM((rows, width), F32)],
        60,
    )(place, slope, *wide, *piece)


def mix_grad(place, hidden_t, wide, extra=None):
    depth, rows = hidden_t.shape
    width = wide[0].shape[2]
    below = 0 if extra is None else extra.shape[1]

    def kernel(p, h_ref, mine_ref, other_ref, *refs):
        term = refs[-1]
        here = pl.multiple_of(p[2] * width, width)
        there = pl.multiple_of((1 - p[2]) * width, width)
        term[0, :depth, pl.ds(here, width)] = dot(h_ref[...], mine_ref[0]).astype(BF)
        term[0, :depth, pl.ds(there, width)] = dot(h_ref[...], other_ref[0]).astype(BF)
        if below:
            term[0, depth:, :] = refs[0][0]

    g_spec = pl.BlockSpec((1, rows, width), lambda c, p: (p[1] ^ c, 0, 0))
    specs = [whole((depth, rows)), g_spec, g_spec]
    args = [hidden_t, *wide]
    if below:
        specs.append(pl.BlockSpec((1, below, 2 * width), lambda c, p: (c, 0, 0)))
        args.append(extra)
    return with_place(
        kernel,
        (4,),
        specs,
        pl.BlockSpec((1, depth + below, 2 * width), lambda c, p: (c, 0, 0)),
        jax.ShapeDtypeStruct((4, depth + below, 2 * width), BF),
        16 * rows * depth * width,
        16 * (rows + depth) * width + 2 * rows * depth,
        (),
        60,
    )(place, *args)


def conv_grad(place, x, gp, shard, side, relative):
    rows, width = x.shape
    images = rows // (side * side)

    def kernel(p, x_ref, gp_ref, o_ref, pad_ref, full_ref):
        mask = block_mask()
        for k in range(width // HALF):
            lanes = slice(k * HALF, (k + 1) * HALF)
            pad_field(x_ref[:, lanes].reshape(side, side, images, HALF), pad_ref)
            turned = gp_ref[:, lanes].T
            for tap in range(TAPS):
                a, b = tap // 3, tap % 3
                square = dot(turned, pad_ref[a : a + side, b : b + side].reshape(rows, HALF)).T
                square = jnp.where(mask, square, 0.0)
                slab = square[:GW]
                for q in range(1, HALF // GW):
                    slab = slab + square[q * GW : (q + 1) * GW]
                full_ref[tap * GW : (tap + 1) * GW, lanes] = slab.astype(BF)
        for plane in range(4):
            index = plane ^ p[0] if relative else plane
            o_ref[index] = full_ref[plane * shard : (plane + 1) * shard, :]

    return with_place(
        kernel,
        (1,),
        [whole((rows, width))] * 2,
        whole((4, shard, width)),
        jax.ShapeDtypeStruct((4, shard, width), BF),
        2 * rows * HALF * width * TAPS,
        rows * width * 4,
        [
            pltpu.VMEM((side + 2, side + 2, images, HALF), BF),
            pltpu.VMEM((4 * shard, width), BF),
        ],
    )(place, x, gp)


def conv_field(gp, w, gradient, side):
    rows, width = gp.shape
    images = rows // (side * side)

    def kernel(gp_ref, w_ref, g_ref, o_ref, pad_ref, wide_ref):
        def put(here, field):
            o_ref[here, :] = (g_ref[here, :].astype(F32) + field).astype(BF)

        grid = gp_ref[...].reshape(side, side, images, HALF)
        convolve_back(grid, w_ref, pad_ref, wide_ref, put)

    half_spec = pl.BlockSpec((rows, HALF), lambda h: (0, h))
    return call(
        kernel,
        jax.ShapeDtypeStruct((rows, width), BF),
        2 * rows * HALF * width * TAPS,
        rows * width * 6,
        grid=(width // HALF,),
        in_specs=[half_spec, pl.BlockSpec((TAPS * GW, HALF), lambda h: (0, h)), half_spec],
        out_specs=half_spec,
        scratch_shapes=[
            pltpu.VMEM((side + 2, side + 2, images, HALF), BF),
            pltpu.VMEM((HALF, TAPS * HALF), BF),
        ],
    )(gp, w, gradient)


def finish(place, scale, last, first, convs, mix_shape, conv_shape):
    layers, depth, width = mix_shape
    _, shard, channels = conv_shape

    def kernel(p, last_ref, first_ref, *refs):
        del p
        mix_ref, conv_ref = refs[-2:]
        mix_ref[1] = last_ref[0].astype(F32) * scale
        mix_ref[0] = first_ref[0, :depth].astype(F32) * scale
        conv_ref[1, : shard // 2] = first_ref[0, depth:, :channels].astype(F32) * scale
        conv_ref[1, shard // 2 :] = first_ref[0, depth:, channels:].astype(F32) * scale
        total = refs[0][0].astype(F32)
        for ref in refs[1:4]:
            total = total + ref[...].astype(F32)
        conv_ref[0] = total * scale

    return with_place(
        kernel,
        (1,),
        [whole((1, depth, width)), whole((1, depth + shard // 2, width)), whole((1, shard, channels))]
        + [whole((shard, channels))] * 3,
        (whole(mix_shape), whole(conv_shape)),
        (jax.ShapeDtypeStruct(mix_shape, F32), jax.ShapeDtypeStruct(conv_shape, F32)),
        0,
        12 * depth * width,
        (),
        32,
    )(place, last, first, *convs)


class Clock:
    def __init__(self, token):
        self.token = token

    def gate(self, value):
        return lax.optimization_barrier((value, self.token))[0]

    def close(self, *values):
        self.token, *values = lax.optimization_barrier((self.token, *values))
        return values


def permute_dp(value, pairs):
    return lax.ppermute(value, "dp", pairs)


def permute_group(value, pairs):
    return lax.ppermute(value, "group", pairs)


def add(*terms):
    total = terms[0].astype(F32)
    for term in terms[1:]:
        total = total + term.astype(F32)
    return total


def gather_outer(own):
    return permute_dp(own, OUTER_INNER)


def gather_inner(own):
    return permute_dp(own, INNER)


def gather_second(a, b):
    return permute_dp(a, INNER), permute_dp(b, OUTWARD)


def gather_third(c):
    return permute_dp(c, OUTWARD)


def scatter_direct(parts):
    return [permute_dp(parts[i], [(j, j ^ i) for j in range(4)]) for i in (1, 2, 3)]


def plane_first(own):
    cut = own.shape[0] // 2
    return permute_group(own[:cut], ACROSS_X), permute_group(own[cut:], ACROSS_Y)


def plane_second(own, first_x, second_y):
    cut = own.shape[0] // 2
    return (
        permute_group(jnp.stack([own[:cut], first_x]), ACROSS_Y),
        permute_group(jnp.stack([own[cut:], second_y]), ACROSS_X),
    )


def plane_join(own, first_x, second_y, first_y, second_x):
    return jnp.stack(
        [
            own,
            jnp.concatenate([first_x, second_x[0]]),
            jnp.concatenate([first_y[0], second_y]),
            jnp.concatenate([first_y[1], second_x[1]]),
        ]
    )


def across_cores(value):
    return permute_group(value, ACROSS_CORE)


def sum_last(base, keep, other, first_x, second_y, first_y, second_x):
    cut = base.shape[0] // 2
    return jnp.concatenate(
        [
            add(base[:cut]) + add(keep[0, :cut], other[0, :cut], first_x[0], first_y),
            add(base[cut:]) + add(keep[0, cut:], other[0, cut:], second_y[0], second_x),
        ]
    ).astype(BF)


def sum_first(keep, other):
    rows = keep.shape[1]
    cut = rows // 2
    first = [add(keep[c, :cut], other[c, :cut]).astype(BF) for c in (1, 3)]
    second = [add(keep[c, cut:], other[c, cut:]).astype(BF) for c in (2, 3)]
    return (
        permute_group(jnp.stack(first), ACROSS_X),
        permute_group(jnp.stack(second), ACROSS_Y),
    )


def sum_second(keep, other, first_x, second_y):
    cut = keep.shape[1] // 2
    return (
        permute_group(add(keep[2, :cut], other[2, :cut], first_x[1]).astype(BF), ACROSS_Y),
        permute_group(add(keep[1, cut:], other[1, cut:], second_y[1]).astype(BF), ACROSS_X),
    )


def staged(images, cotangent, conv_weight, mix_weight):
    batch, side, _, width = images.shape
    shard = conv_weight.shape[1]
    rows = batch * side * side
    scale = 1.0 / math.sqrt(rows * lax.axis_size("dp"))
    z = lax.axis_index("dp")
    group = lax.axis_index("group")
    place = place_vector(z, group // 2, group % 2)
    clock = Clock(z)
    gate, close = clock.gate, clock.close

    def to_rows(field):
        return field.transpose(1, 2, 0, 3).reshape(rows, width)

    def from_rows(flat):
        return flat.reshape(side, side, batch, width).transpose(2, 0, 1, 3)

    tall = (shard // 2 + 15) // 16 * 16

    def with_kernels(weights, layer):
        kernels = conv_weight[layer]
        below = jnp.concatenate([kernels[:tall], kernels[shard - tall :]], axis=1)
        return jnp.concatenate([weights, below])

    depth = width // 2
    own0 = with_kernels(mix_weight[0], 0)
    own1, own2 = with_kernels(mix_weight[1, :depth], 1), mix_weight[1, depth:]
    a0, b0 = gather_outer(own0), gather_inner(own0)
    far0 = permute_dp(conv_weight[0], [(0, 3), (3, 0)])
    x0 = to_rows(images)
    g2 = to_rows(cotangent)
    a0, b0, far0, x0, g2 = close(a0, b0, far0, x0, g2)

    wide2 = lax.all_gather(gate(g2), "group", axis=0)
    c0, d0 = gather_second(a0, b0)
    c0, d0 = close(c0, d0)

    e0 = gather_third(c0[:width])
    b1, b2 = gather_inner(gate(own1)), gather_inner(gate(own2))
    sent, keep, hidden0, hidden0_t, slope0, conv0 = first_layer(
        place, x0, (own0, a0, b0, c0, d0), far0, side
    )
    e0, b1, b2, sent, keep, hidden0, hidden0_t, slope0, conv0 = close(
        e0, b1, b2, sent, keep, hidden0, hidden0_t, slope0, conv0
    )
    p0 = (own0, a0, b0, c0, d0, e0)

    a1 = gather_outer(gate(own1))
    other = across_cores(sent)
    sent_last, keep_last = last_slot(place, hidden0, b0, e0)
    other_last = across_cores(sent_last)
    a1, other, keep_last, other_last = close(a1, other, keep_last, other_last)

    c1, d1 = gather_second(a1, b1)
    a2 = gather_outer(gate(own2))
    to_x, to_y, near, first_far, second_far = sum_cores(place, keep, keep_last, other, other_last)
    sx, sy = permute_group(to_x, ACROSS_X), permute_group(to_y, ACROSS_Y)
    c1, d1, a2, sx, sy = close(c1, d1, a2, sx, sy)

    e1 = gather_third(c1)
    c2 = gather_inner(a2)
    ty = permute_group(add(first_far, sx[1]).astype(BF), ACROSS_Y)
    tx = permute_group(add(second_far, sy[1]).astype(BF), ACROSS_X)
    ty, tx, e1, c2 = close(ty, tx, e1, c2)
    p1 = (own1, a1, b1, c1, d1, e1)

    d2 = gather_third(gate(b2))
    e2 = gather_third(c2)
    x1, hidden1, slope1, conv1, m1 = next_layer(
        place, x0, near, sx, sy, ty, tx, p1, depth, wide2, side
    )
    last = lax.psum_scatter(m1, "dp", scatter_dimension=0, tiled=True)
    x1, hidden1, slope1, conv1, d2, e2 = close(x1, hidden1, slope1, conv1, d2, e2)
    p2 = (own2, a2, b2, c2, d2, e2)

    gp1, g1 = output_gradient(place, wide2, [p1, p2], slope1, conv1, g2, side)
    ax, ay = plane_first(g1)
    gp1, g1, ax, ay = close(gp1, g1, ax, ay)
    ayy, axx = plane_second(g1, ax, ay)
    mine = plane_join(g1, ax, ay, ayy, axx)
    terms1 = conv_grad(place, x1, gp1, shard, side, False)
    mine, terms1 = close(mine, terms1)
    wide1 = (mine, across_cores(mine))
    below = jnp.concatenate([terms1[:, : shard // 2], terms1[:, shard // 2 :]], axis=2)
    m0 = mix_grad(place, hidden0_t, wide1, below)
    m0, last = close(m0, last)
    first = lax.psum_scatter(m0, "dp", scatter_dimension=0, tiled=True)

    gp0 = grad_pre(place, wide1, p0, slope0)
    terms0 = conv_grad(place, x0, gp0, shard, side, True)
    gp0, terms0 = close(gp0, terms0)
    cs = scatter_direct(terms0)

    sent, keep = mix_columns(place, gate(hidden1), [p1, p2])
    other = across_cores(sent)
    keep, other = close(keep, other)
    sx, sy = sum_first(keep, other)
    g0 = conv_field(gp0, conv0, g1, side)
    sx, sy, g0, *cs = close(sx, sy, g0, *cs)
    ty, tx = sum_second(keep, other, sx, sy)
    features = from_rows(sum_last(x1, keep, other, sx, sy, ty, tx))
    grad_images = from_rows(g0)
    grad_mix, grad_conv = finish(
        place, scale, last, first, [terms0, *cs], mix_weight.shape, conv_weight.shape
    )
    return features, grad_images, grad_conv, grad_mix


def make_patches(field):
    side_cells = field.shape[1]
    padded = jnp.pad(field, ((0, 0), (1, 1), (1, 1), (0, 0)))
    tap_list = [
        padded[:, row_shift : row_shift + side_cells, col_shift : col_shift + side_cells, :]
        for row_shift in range(3)
        for col_shift in range(3)
    ]
    return jnp.stack(tap_list, axis=3).reshape(-1, 9, field.shape[3])


def fold_patches(pieces, batch_size, side_cells):
    pieces = pieces.reshape(batch_size, side_cells, side_cells, 9, pieces.shape[2])
    summed = jnp.zeros((batch_size, side_cells + 2, side_cells + 2, pieces.shape[4]), F32)
    for tap_index in range(9):
        row_shift = tap_index // 3
        col_shift = tap_index % 3
        summed = summed + jnp.pad(
            pieces[:, :, :, tap_index, :],
            ((0, 0), (row_shift, 2 - row_shift), (col_shift, 2 - col_shift), (0, 0)),
        )
    return summed[:, 1 : side_cells + 1, 1 : side_cells + 1, :]


def silu_slope(value):
    sigmoid_v = jax.nn.sigmoid(value)
    return sigmoid_v * (1.0 + value * (1.0 - sigmoid_v))


def general(images, cotangent, conv_weight, mix_weight):
    batch_size, side_cells, _, local_width = images.shape
    local_groups = local_width // GW
    row_count = batch_size * side_cells * side_cells
    layer_count = conv_weight.shape[0]
    grad_scale = 1.0 / math.sqrt(row_count * lax.axis_size("dp"))
    fetched = [
        (
            lax.all_gather(conv_weight[layer], "dp", axis=0, tiled=True),
            lax.all_gather(mix_weight[layer], "dp", axis=1, tiled=True),
        )
        for layer in range(layer_count)
    ]
    current = images
    saved = []
    for layer in range(layer_count):
        conv_full, mix_full = fetched[layer]
        tap_weights = conv_full.reshape(9 * GW, local_groups, GW).transpose(1, 0, 2)
        flat = make_patches(current).reshape(row_count, 9, local_groups, GW)
        patches = flat.transpose(0, 2, 1, 3).reshape(row_count, local_groups, 9 * GW)
        pre_act = jnp.einsum(
            "pgk,gko->pgo", patches, tap_weights, preferred_element_type=F32
        ).reshape(row_count, local_width)
        hidden = jax.nn.silu(pre_act).astype(BF)
        mixed = lax.psum_scatter(
            jnp.dot(hidden, mix_full, preferred_element_type=F32).astype(BF),
            "group",
            scatter_dimension=1,
            tiled=True,
        ).astype(F32)
        saved.append((patches, pre_act, hidden, tap_weights, mix_full))
        current = (
            (current.reshape(row_count, local_width).astype(F32) + mixed)
            .astype(BF)
            .reshape(images.shape)
        )
    gradient = cotangent
    conv_grads = []
    mix_grads = []
    for layer in reversed(range(layer_count)):
        patches, pre_act, hidden, tap_weights, mix_full = saved[layer]
        flat_grad = gradient.reshape(row_count, local_width)
        grad_wide = lax.all_gather(flat_grad, "group", axis=1, tiled=True)
        mix_term = lax.dot_general(
            hidden, grad_wide, (((0,), (0,)), ((), ())), preferred_element_type=F32
        )
        grad_hidden = dot_nt(grad_wide, mix_full)
        grad_pre = (
            (grad_hidden * silu_slope(pre_act)).astype(BF).reshape(row_count, local_groups, GW)
        )
        conv_term = jnp.einsum("pgk,pgo->gko", patches, grad_pre, preferred_element_type=F32)
        conv_term = conv_term.transpose(1, 0, 2).reshape(9 * GW, local_width)
        patch_grad = jnp.einsum("pgo,gko->pgk", grad_pre, tap_weights, preferred_element_type=F32)
        patch_grad = (
            patch_grad.reshape(row_count, local_groups, 9, GW)
            .transpose(0, 2, 1, 3)
            .reshape(row_count, 9, local_width)
        )
        field_grad = fold_patches(patch_grad, batch_size, side_cells)
        conv_summed, mix_summed = (
            lax.psum_scatter(
                conv_term.astype(BF), "dp", scatter_dimension=0, tiled=True
            ).astype(F32),
            lax.psum_scatter(
                mix_term.astype(BF), "dp", scatter_dimension=1, tiled=True
            ).astype(F32),
        )
        conv_grads.insert(0, conv_summed * grad_scale)
        mix_grads.insert(0, mix_summed * grad_scale)
        gradient = (gradient.astype(F32) + field_grad).astype(BF)
    return (current, gradient, jnp.stack(conv_grads), jnp.stack(mix_grads))


def solution(mesh):
    fits = mesh.shape["dp"] == 4 and mesh.shape["group"] == 8
    return jax.shard_map(
        staged if fits else general,
        mesh=mesh,
        in_specs=(
            P("dp", None, None, "group"),
            P("dp", None, None, "group"),
            P(None, "dp", "group"),
            P(None, "group", "dp"),
        ),
        out_specs=(
            P("dp", None, None, "group"),
            P("dp", None, None, "group"),
            P(None, "dp", "group"),
            P(None, "group", "dp"),
        ),
        check_vma=False,
    )
```
